128 devices in a mesh: gx: 8 (over x, core), gy: 16 (over y, z).
Axes of the slice: x: 4, y: 4, z: 4, core: 2. Of those that a mesh axis runs over, the one named last changes fastest.
Arguments:
- right_side: float32 [256, 512, 512], P('gx', 'gy'), may hold values from -120 to 120
- absorption: float32 [256, 512, 512], P('gx', 'gy'), may hold values from 0.001 to 0.05
Outputs:
- solution: float32 [256, 512, 512], P('gx', 'gy')
The draws below stay inside these ranges and needn't reach their ends.
All inputs are finite; a program needn't handle non-finite values.
Results may differ from the reference program's by a relative error of at most 0.00002.
Values sent between devices are 32-bit elements; how exact they have to be, the bound alone decides.
A program may use at most 128 MiB of HBM per device.

```python
import math
from functools import partial
import jax
import jax.numpy as jnp
from jax import lax

LEVELS = 6
DEGREE = 4
NX = 256
NY = 512
NZ = 512


def draw_right_side(key, part):
    key = jax.random.fold_in(key, 11)
    sample = 20.0 * jax.random.normal(key, (NX, NY, NZ), jnp.float32) + 15.0
    return jnp.clip(sample, -120.0, 120.0)


def block_levels(stream_key, dims, shards, low, largest):
    def one(axis_at, parts):
        draws = jax.random.uniform(jax.random.fold_in(jax.random.fold_in(stream_key, 6), axis_at), (parts,), jnp.float32, low / len(shards), largest / len(shards))
        return jnp.repeat(jnp.exp(draws), dims[axis_at] // parts).reshape((-1,) + (1,) * (len(dims) - axis_at - 1))

    level = one(*shards[0])
    for cut in shards[1:]:
        level = level * one(*cut)
    return level


def setup_inputs(seed: int = 0) -> dict:
    streams_of = jax.random.split(jax.random.key(seed), 3)
    right_side = draw_right_side(jax.random.fold_in(streams_of[2], 71), 0)
    absorption = jnp.clip(jnp.exp(math.log(0.05) - 3.912023 * jax.random.uniform(streams_of[1], (NX, NY, NZ), jnp.float32) ** block_levels(streams_of[1], (NX, NY, NZ), ((0, 8), (1, 16)), -0.2, 0.2)), 0.001, 0.05)
    return {"right_side": right_side, "absorption": absorption}


center_value = 0.7875
half_width = 0.6125


def box_total(padded):
    along_x = padded[:-2] + padded[1:-1] + padded[2:]
    along_y = along_x[:, :-2] + along_x[:, 1:-1] + along_x[:, 2:]
    return along_y[:, :, :-2] + along_y[:, :, 1:-1] + along_y[:, :, 2:]


def apply_op(field, diagonal):
    padded = jnp.pad(field, 1)
    return (diagonal + 1.0) * field - box_total(padded)


def chebyshev(start, source, diagonal, operate):
    if start is None:
        residue = source / diagonal
    else:
        residue = (source - operate(start)) / diagonal
    update = residue / center_value
    ratio = half_width / center_value
    field = start
    for iteration in range(DEGREE):
        field = update if field is None else field + update
        if iteration < DEGREE - 1:
            residue = residue - operate(update) / diagonal
            ratio_next = 1.0 / (2.0 * center_value / half_width - ratio)
            update = (ratio_next * ratio) * update + (2.0 * ratio_next / half_width) * residue
            ratio = ratio_next
    return field


def restrict_dim(field, dim, border):
    count = field.shape[dim]
    joined = jnp.concatenate([field, border], axis=dim)
    first = lax.slice_in_dim(joined, 0, count, 2, dim)
    middle = lax.slice_in_dim(joined, 1, count, 2, dim)
    last = lax.slice_in_dim(joined, 2, count + 1, 2, dim)
    return 0.25 * first + 0.5 * middle + 0.25 * last


def prolong_dim(coarse, dim, border):
    count = coarse.shape[dim]
    joined = jnp.concatenate([border, coarse], axis=dim)
    before = lax.slice_in_dim(joined, 0, count, 1, dim)
    even_part = 0.5 * (before + coarse)
    stacked = jnp.stack([even_part, coarse], axis=dim + 1)
    new_shape = list(coarse.shape)
    new_shape[dim] = 2 * count
    return stacked.reshape(new_shape)


def edge_zeros(field, dim):
    return jnp.zeros_like(lax.slice_in_dim(field, 0, 1, 1, dim))


def restrict_all(field):
    for dim in range(3):
        field = restrict_dim(field, dim, edge_zeros(field, dim))
    return field


def prolong_all(field):
    for dim in range(3):
        field = prolong_dim(field, dim, edge_zeros(field, dim))
    return field


def vcycle(depth_level, source, absorption):
    diagonal = 26.0 + absorption
    operate = partial(apply_op, diagonal=diagonal)
    field = chebyshev(None, source, diagonal, operate)
    if depth_level < LEVELS - 1:
        residue = source - operate(field)
        coarse_source = 4.0 * restrict_all(residue)
        coarse_absorb = 4.0 * restrict_all(absorption)
        field = field + prolong_all(vcycle(depth_level + 1, coarse_source, coarse_absorb))
    return chebyshev(field, source, diagonal, operate)


def reference(right_side, absorption):
    return vcycle(0, right_side, absorption)
```

```python
import jax
import jax.numpy as jnp
from jax import lax
from jax.experimental import pallas as pl
from jax.experimental.pallas import tpu as pltpu
from jax.sharding import PartitionSpec as P

MESH = pl.DeviceIdType.MESH
CENTER = 0.7875
HALF = 0.6125
GX, GY = 8, 16
X0, Y0 = 4, 12
LO, UP = 4, 5
B = (32, 16, 8)
ZT = (4, 2, 1)
ROWS = (56, 40, 40)
CH = (5, 3, 2)
DIRS = [(dx, dy) for dx in (-1, 0, 1) for dy in (-1, 0, 1) if dx or dy]
F32 = jnp.float32


def chebyshev_factors():
    out, q = [], HALF / CENTER
    for _ in range(3):
        n = 1.0 / (2.0 * CENTER / HALF - q)
        out.append((n * q, 2.0 * n / HALF))
        q = n
    return out


FACTORS = chebyshev_factors()


def device(dx, dy):
    return (
        lax.rem(lax.axis_index("gx") + (dx + GX), GX),
        lax.rem(lax.axis_index("gy") + (dy + GY), GY),
    )


def dot(a, b):
    return jnp.dot(a, b, precision=lax.Precision.HIGHEST, preferred_element_type=F32)


def spans(way, width, lo, up, start):
    if way == 0:
        return (start, width), (start, width)
    if way > 0:
        return (start + width - lo, lo), (start - lo, lo)
    return (start, up), (start + width, up)


class Exchange:
    def __init__(self, ref, width, lo, up, send, recv, slot):
        self.copies = []
        for n, (dx, dy) in enumerate(DIRS):
            (sx, nx), (tx, _) = spans(dx, width, lo, up, X0)
            (sy, ny), (ty, _) = spans(dy, width, lo, up, Y0)
            self.copies.append(
                pltpu.make_async_remote_copy(
                    src_ref=ref.at[pl.ds(sx, nx), :, pl.ds(sy, ny), :],
                    dst_ref=ref.at[pl.ds(tx, nx), :, pl.ds(ty, ny), :],
                    send_sem=send.at[slot, n],
                    recv_sem=recv.at[slot, n],
                    device_id=device(dx, dy),
                    device_id_type=MESH,
                )
            )

    def start(self):
        for c in self.copies:
            c.start()
        return self

    def wait_recv(self):
        for c in self.copies:
            c.wait_recv()

    def wait_send(self):
        for c in self.copies:
            c.wait_send()


def zero_outside(ref, width, lower=True, upper=True):
    gx, gy = lax.axis_index("gx"), lax.axis_index("gy")

    def clear(cond, planes, rows):
        @pl.when(cond)
        def _():
            view = (pl.ds(*planes), slice(None), pl.ds(*rows), slice(None))
            ref[view] = jnp.zeros((planes[1], ref.shape[1], rows[1], 128), F32)

    whole_x, whole_y = (0, X0 + width + UP), (8, width + 9)
    if lower:
        clear(gx == 0, (0, X0), whole_y)
        clear(gy == 0, whole_x, (8, 4))
    if upper:
        clear(gx == GX - 1, (X0 + width, UP), whole_y)
        clear(gy == GY - 1, whole_x, (Y0 + width, UP))


def lanes_of(u):
    return lax.broadcasted_iota(jnp.int32, u.shape, u.ndim - 1)


def z_split(u):
    lane = lanes_of(u)
    left, right = pltpu.roll(u, 1, axis=2), pltpu.roll(u, 127, axis=2)
    zero = jnp.zeros_like(u[:1])
    if u.shape[0] > 1:
        before = jnp.concatenate([zero, left[:-1]], 0)
        after = jnp.concatenate([right[1:], zero], 0)
    else:
        before = after = zero
    return u + jnp.where(lane == 0, before, left) + jnp.where(lane == 127, after, right)


def z_halves(u):
    lane = lanes_of(u) & 63
    left, right = pltpu.roll(u, 1, axis=2), pltpu.roll(u, 127, axis=2)
    return u + jnp.where(lane == 0, 0.0, left) + jnp.where(lane == 63, 0.0, right)


def z_open(u):
    return u + pltpu.roll(u, 1, axis=2) + pltpu.roll(u, 127, axis=2)


def x_plain(p, n):
    out = []
    for k in range(0, n, 2):
        m = p[k + 1] + p[k + 2] if k + 1 < n else p[k + 1] + p[k + 2]
        out.append(p[k] + m)
        if k + 1 < n:
            out.append(m + p[k + 3])
    return out


def x_pairs(p, n):
    w = [pltpu.roll(v, 64, axis=2) for v in p]
    low = lanes_of(p[0]) < 64
    return [p[k + 1] + w[k + 1] + jnp.where(low, w[k], w[k + 2]) for k in range(n)]


def smooth_step(lev, src, r, x_range, dst=None, al=0.0, be=0.0, r_out=None, extra=None):
    gi, tmp = lev["gi"], lev["tmp"]
    rows = 8 * (lev["ch"] + 2)

    def group(x, n):
        p = [src[x - 1 + k, :, 0:rows, :] for k in range(n + 2)]
        for k, s in enumerate(lev["xsum"](p, n)):
            tmp[k] = s
        for k in range(n):
            for c in range(lev["ch"]):
                a = 8 + 8 * c
                u = tmp[k, :, a - 1 : a + 7, :] + tmp[k, :, a : a + 8, :] + tmp[k, :, a + 1 : a + 9, :]
                box = lev["zsum"](u)
                d = src[x + k, :, a : a + 8, :]
                new = (r[x + k, :, a : a + 8, :] - d) + gi[x + k, :, a : a + 8, :] * (box - d)
                if extra is not None:
                    extra(x + k, a, d, new)
                if r_out is not None:
                    r_out[x + k, :, a : a + 8, :] = new
                if dst is not None:
                    dst[x + k, :, a : a + 8, :] = al * d + be * new

    first, last = x_range
    size = tmp.shape[0]
    full = (last - first) // size
    rest = (last - first) - full * size
    if full == 1:
        group(first, size)
    elif full:
        def body(i, carry):
            group(first + i * size, size)
            return carry
        lax.fori_loop(0, full, body, 0)
    if rest:
        group(first + full * size, rest)


def begin(lev, f, s, planes, chunks, mask):
    gi, r, d = lev["gi"], lev["r"], lev["d"][0]

    def body(x, carry):
        for c in range(chunks):
            a = 8 + 8 * c
            g = mask(1.0 / (26.0 + s[x, :, a : a + 8, :]), x, a)
            gi[x, :, a : a + 8, :] = g
            new = f[x, :, a : a + 8, :] * g
            r[x, :, a : a + 8, :] = new
            d[x, :, a : a + 8, :] = new * (1.0 / CENTER)
        return carry

    lax.fori_loop(planes[0], planes[1], body, 0)


def store_own(ref, x, a, value, width):
    lo, hi = max(a, Y0), min(a + 8, Y0 + width)
    if lo < hi:
        ref[x, :, lo:hi, :] = value[:, lo - a : hi - a, :]


def restrict_rows(src, tmp, out, count, cy, first_plane, first_row, rows):
    size = min(4, count)

    def body(i, carry):
        for k in range(size):
            x = first_plane + 2 * (i * size + k)
            tmp[k] = 0.25 * (src[x, :, 0:rows, :] + src[x + 2, :, 0:rows, :]) + 0.5 * src[x + 1, :, 0:rows, :]
        for k in range(size):
            for z in range(src.shape[1]):
                v = 0.25 * (
                    tmp[k, z, pl.ds(first_row, cy, stride=2), :]
                    + tmp[k, z, pl.ds(first_row + 2, cy, stride=2), :]
                ) + 0.5 * tmp[k, z, pl.ds(first_row + 1, cy, stride=2), :]
                at = (i * size + k) * cy
                if cy % 8 == 0:
                    at = pl.multiple_of(at, 8)
                out[z, pl.ds(at, cy), :] = v
        return carry

    lax.fori_loop(0, count // size, body, 0)


def split_restrict(level, src, tmp, mid, matrix, target):
    cb = B[level + 1]
    restrict_rows(src, tmp, mid, cb, cb, X0, Y0, 8 * (CH[level] + 2))
    total = None
    for z in range(ZT[level]):
        part = dot(mid[z], matrix[z])
        total = part if total is None else total + part
    for i in range(cb):
        for z in range(ZT[level + 1]):
            target[X0 + i, z, Y0 : Y0 + cb, :] = total[i * cb : (i + 1) * cb, 128 * z : 128 * z + 128]


def interleave(ez, target, count, t0, rows, nj, first_plane, first_row):
    for_z = range(target.shape[1])

    def body(i, carry):
        t = t0 + i
        for z in for_z:
            a1, b1 = ez[t, z, rows : rows + nj, :], ez[t, z, rows - 1 : rows - 1 + nj, :]
            a0, b0 = ez[t - 1, z, rows : rows + nj, :], ez[t - 1, z, rows - 1 : rows - 1 + nj, :]
            odd, even = a1, 0.5 * (a1 + b1)
            odd_0, even_0 = a0, 0.5 * (a0 + b0)
            x = first_plane + 2 * i
            target[x, z, pl.ds(first_row + 1, nj, stride=2), :] = 0.5 * (odd_0 + odd)
            target[x, z, pl.ds(first_row, nj, stride=2), :] = 0.5 * (even_0 + even)
            target[x + 1, z, pl.ds(first_row + 1, nj, stride=2), :] = odd
            target[x + 1, z, pl.ds(first_row, nj, stride=2), :] = even
        return carry

    lax.fori_loop(0, count, body, 0)


def kernel(f_hbm, s_hbm, out_hbm, *refs):
    it = iter(refs)
    lev = []
    for l in range(3):
        me = dict(ch=CH[l], xsum=x_plain, zsum=z_split)
        for name in ("r", "s", "rho", "tmp", "mid") + (("e",) if l else ()):
            me[name] = next(it)
        if l == 1:
            old = lev[0]["d"]
            views = [old[n].at[pl.ds(0, 25), pl.ds(z, 2), pl.ds(0, 40), :] for n in (2, 3, 1) for z in (0, 2)]
            me["d"], me["gi"], me["x"] = views[:4], views[4], views[5]
        else:
            me["d"] = [next(it) for _ in range(4)]
            me["gi"], me["x"] = next(it), next(it)
        me["ez"] = me["d"][1].at[pl.ds(0, 21), :, pl.ds(0, 32), :] if l == 0 else next(it)
        lev.append(me)
    for l in range(3, 6):
        me = dict(ch=(8, 4, 2)[l - 3], xsum=x_pairs if l == 3 else x_plain, zsum=z_halves if l == 3 else z_open)
        for name in ("gi", "tmp", "mid", "ez"):
            me[name] = next(it)
        if l == 4:
            old = lev[0]["r"]
            fields = [old.at[pl.ds(x, 18), pl.ds(z, 1), pl.ds(0, 48), :] for x in (0, 18) for z in range(4)]
        else:
            fields = [next(it) for _ in range(8)]
        me["d"] = fields[:4]
        me["r"], me["s"], me["x"], me["f"] = fields[4:]
        lev.append(me)
    blk_f, blk_s = next(it), next(it)
    rz0, pz0, rz1, pz1, rz2, pz2, rz3, pz3, rz4, pz4 = [next(it) for _ in range(10)]
    load_sem, send, recv, gsend, grecv = [next(it) for _ in range(5)]
    gx, gy = lax.axis_index("gx"), lax.axis_index("gy")

    loads = []
    for n, (hbm, ref) in enumerate(((s_hbm, lev[0]["s"]), (f_hbm, lev[0]["r"]))):
        for z in range(4):
            c = pltpu.make_async_copy(
                hbm.at[:, :, pl.ds(128 * z, 128)], ref.at[pl.ds(X0, 32), z, pl.ds(Y0, 32), :], load_sem.at[n, z]
            )
            c.start()
            loads.append(c)

    def clear_pads(l):
        for ref in lev[l]["d"] + [lev[l]["r"], lev[l]["s"], lev[l]["x"]]:
            rows = ref.shape[2]
            top = 8 + 8 * lev[l]["ch"]
            off = 2 if l == 3 else 1
            n = ref.shape[0]
            ref[0:off] = jnp.zeros((off,) + ref.shape[1:], F32)
            ref[n - off : n] = jnp.zeros((off,) + ref.shape[1:], F32)
            ref[:, :, 0:8, :] = jnp.zeros((n, 1, 8, 128), F32)
            ref[:, :, top:rows, :] = jnp.zeros((n, 1, rows - top, 128), F32)
        ez = lev[l]["ez"]
        ez[...] = jnp.zeros(ez.shape, F32)
        mid = lev[l]["mid"]
        mid[...] = jnp.zeros(mid.shape, F32)

    clear_pads(3)
    clear_pads(5)

    barrier = pltpu.get_barrier_semaphore()
    peers = list(DIRS) + [(d, 0) for d in range(2, GX - 1)] + [(0, d) for d in range(2, GY - 1)]
    for dx, dy in peers:
        pl.semaphore_signal(barrier, inc=1, device_id=device(dx, dy), device_id_type=MESH)
    pl.semaphore_wait(barrier, len(peers))

    for c in loads[:4]:
        c.wait()
    slot = iter(range(16))

    def exchange(ref, l, lo, up):
        return Exchange(ref, B[l], lo, up, send, recv, next(slot)).start()

    sends = []
    ex_s = [exchange(lev[0]["s"], 0, LO, UP)]
    for c in loads[4:]:
        c.wait()
    ex_f = exchange(lev[0]["r"], 0, LO, UP)

    def fill(ref, index, fn):
        shape = ref.shape[1:]
        ref[index] = fn(lax.broadcasted_iota(jnp.int32, shape, 0), lax.broadcasted_iota(jnp.int32, shape, 1))

    def wr(z, k):
        return jnp.where(z == 2 * k + 1, 2.0, jnp.where((z == 2 * k) | (z == 2 * k + 2), 1.0, 0.0))

    def wp(k, z):
        return jnp.where(z == 2 * k + 1, 1.0, jnp.where((z == 2 * k) | (z == 2 * k + 2), 0.5, 0.0))

    for t in range(4):
        fill(rz0, t, lambda z, k: wr(z + 128 * t, k))
    for t in range(2):
        fill(pz0, t, lambda k, z: wp(k + 128 * t, z))
        fill(rz1, t, lambda z, k: wr(z + 128 * t, k))
    fill(pz1, 0, wp)
    for h in range(2):
        fill(rz2, h, lambda z, k: jnp.where((k >> 6) == h, wr(z, k & 63), 0.0))
        fill(pz2, h, lambda k, z: jnp.where((k >> 6) == h, wp(k & 63, z), 0.0))
    fill(rz3, 0, lambda z, k: jnp.where(k < 32, wr(z & 63, k) * jnp.where(z < 64, 0.25, 0.5), 0.0))
    fill(rz3, 1, lambda z, k: jnp.where((k < 32) & (z < 64), wr(z, k) * 0.25, 0.0))
    fill(pz3, 0, lambda k, z: jnp.where(k < 32, wp(k, z & 63) * jnp.where(z < 64, 0.5, 1.0), 0.0))
    fill(pz3, 1, lambda k, z: jnp.where((k < 32) & (z < 64), wp(k, z) * 0.5, 0.0))
    fill(rz4, 0, lambda z, k: jnp.where((k < 16) & (z < 32), wr(z, k), 0.0))
    fill(pz4, 0, lambda k, z: jnp.where((k < 16) & (z < 32), wp(k, z), 0.0))
    rz, pz = (rz0, rz1), (pz0, pz1)

    def pack_block(l2, src, blk):
        mid = l2["mid"]
        restrict_rows(src, l2["tmp"], mid, 4, 4, X0, Y0, 32)
        lo, hi = dot(mid[0], rz2[0]), dot(mid[0], rz2[1])
        for i in range(2):
            blk[i, 0, 0:4, :] = lo[8 * i : 8 * i + 4] + hi[8 * i + 4 : 8 * i + 8]

    class Gather:
        def __init__(self, n, blk, ref):
            own = ref.at[pl.ds(2 + 2 * gx, 2), :, pl.ds(8 + 4 * gy, 4), :]
            src = blk.at[:, :, pl.ds(0, 4), :]
            self.local = pltpu.make_async_copy(src, own, load_sem.at[2, n])
            slab = ref.at[pl.ds(2, 16), :, pl.ds(8 + 4 * gy, 4), :]
            self.first = [
                pltpu.make_async_remote_copy(
                    src_ref=src, dst_ref=own, send_sem=gsend.at[n, d], recv_sem=grecv.at[n, d],
                    device_id=device(d, 0), device_id_type=MESH)
                for d in range(1, GX)
            ]
            self.second = [
                pltpu.make_async_remote_copy(
                    src_ref=slab, dst_ref=slab, send_sem=gsend.at[n, 8 + d], recv_sem=grecv.at[n, 8 + d],
                    device_id=device(0, d), device_id_type=MESH)
                for d in range(1, GY)
            ]

        def start(self):
            for c in self.first:
                c.start()
            self.local.start()

        def middle(self):
            self.local.wait()
            for c in self.first:
                c.wait_recv()
            for c in self.second:
                c.start()

        def finish(self):
            for c in self.second:
                c.wait_recv()

        def wait_send(self):
            for c in self.first + self.second:
                c.wait_send()

    gather_s = Gather(0, blk_s, lev[3]["s"])
    gather_f = Gather(1, blk_f, lev[3]["f"])

    def edge_mask(l):
        row_lo = jnp.where(gy == 0, Y0, 0)
        row_hi = jnp.where(gy == GY - 1, Y0 + B[l], 1000)
        x_lo = jnp.where(gx == 0, X0, 0)
        x_hi = jnp.where(gx == GX - 1, X0 + B[l], 1000)

        def mask(v, x, a):
            row = lax.broadcasted_iota(jnp.int32, v.shape, 1) + a
            inside = (row >= row_lo) & (row < row_hi) & (x >= x_lo) & (x < x_hi)
            return jnp.where(inside, v, 0.0)

        return mask

    def pre(l, between):
        me, b = lev[l], B[l]
        begin(me, me["r"], me["s"], (0, b + 9), me["ch"] + 1, edge_mask(l))
        d, r = me["d"], me["r"]
        for k in range(3):
            al, be = FACTORS[k]
            smooth_step(me, d[k], r, (X0 - 3 + k, X0 + b + 4 - k), d[k + 1], al, be, r_out=r)
            between(k)

        def residual(x, a, _, new):
            r[x, :, a : a + 8, :] = (26.0 + me["s"][x, :, a : a + 8, :]) * new

        def extra(x, a, dd, new):
            residual(x, a, dd, new)
            store_own(me["rho"], x, a, new, b)
            me["x"][x - X0, :, a : a + 8, :] = (
                (d[0][x, :, a : a + 8, :] + d[1][x, :, a : a + 8, :]) + d[2][x, :, a : a + 8, :]
            ) + dd

        smooth_step(me, d[3], r, (X0, X0 + b), extra=extra)
        smooth_step(me, d[3], r, (X0 + b, X0 + b + 1), extra=residual)

    def post(l, emit):
        me, b = lev[l], B[l]
        d, rho = me["d"], me["rho"]
        smooth_step(me, d[0], rho, (X0 - 3, X0 + b + 3), d[1], 0.0, 1.0 / CENTER, r_out=rho)
        smooth_step(me, d[1], rho, (X0 - 2, X0 + b + 2), d[2], *FACTORS[0], r_out=rho)
        smooth_step(me, d[2], rho, (X0 - 1, X0 + b + 1), d[3], *FACTORS[1], r_out=rho)
        al, be = FACTORS[2]

        def extra(x, a, dd, new):
            s = slice(a, a + 8)
            total = (me["x"][x - X0, :, s, :] + d[0][x, :, s, :]) + (d[1][x, :, s, :] + d[2][x, :, s, :])
            emit(x, a, (total + dd) + (al * dd + be * new))

        smooth_step(me, d[3], rho, (X0, X0 + b), extra=extra)

    def coarse_s(k):
        if k < 2:
            ex_s[k + 1].wait_recv()
            zero_outside(lev[k + 1]["s"], B[k + 1])
        if k == 0:
            split_restrict(1, lev[1]["s"], lev[1]["tmp"], lev[1]["mid"], rz[1], lev[2]["s"])
            ex_s.append(exchange(lev[2]["s"], 2, LO, UP))
        elif k == 1:
            pack_block(lev[2], lev[2]["s"], blk_s)
            gather_s.start()
        else:
            gather_s.middle()

    ex_s[0].wait_recv()
    zero_outside(lev[0]["s"], 32)
    split_restrict(0, lev[0]["s"], lev[0]["tmp"], lev[0]["mid"], rz[0], lev[1]["s"])
    ex_s.append(exchange(lev[1]["s"], 1, LO, UP))

    ex_rho = []
    for l in range(3):
        ex_f.wait_recv()
        ex_f.wait_send()
        pre(l, coarse_s if l == 0 else lambda k: None)
        ex_rho.append(exchange(lev[l]["rho"], l, 3, 3))
        if l < 2:
            split_restrict(l, lev[l]["r"], lev[l]["tmp"], lev[l]["mid"], rz[l], lev[l + 1]["r"])
            ex_f = exchange(lev[l + 1]["r"], l + 1, LO, UP)
    pack_block(lev[2], lev[2]["r"], blk_f)
    gather_f.start()
    clear_pads(4)
    gather_f.middle()
    gather_s.finish()
    gather_f.finish()

    def whole_pre(l, off, planes):
        me = lev[l]
        d, r = me["d"], me["r"]
        lanes = (128, 32, 16)[l - 3]

        def mask(v, x, a):
            return v if lanes == 128 else jnp.where(lanes_of(v) < lanes, v, 0.0)

        begin(me, me["f"], me["s"], (off, off + planes), me["ch"], mask)
        for k in range(3):
            al, be = FACTORS[k]
            smooth_step(me, d[k], r, (off, off + planes), d[k + 1], al, be, r_out=r)

    def whole_residual(l, off, planes, f):
        me = lev[l]
        d, r = me["d"], me["r"]

        def extra(x, a, dd, new):
            s = slice(a, a + 8)
            me["x"][x, :, s, :] = ((d[0][x, :, s, :] + d[1][x, :, s, :]) + d[2][x, :, s, :]) + dd
            f[x, :, s, :] = (26.0 + me["s"][x, :, s, :]) * new

        smooth_step(me, d[3], r, (off, off + planes), r_out=r, extra=extra)

    def whole_post(l, off, planes):
        me = lev[l]
        d, r = me["d"], me["r"]
        span = (off, off + planes)
        smooth_step(me, d[0], r, span, d[1], 0.0, 1.0 / CENTER, r_out=r)
        smooth_step(me, d[1], r, span, d[2], *FACTORS[0], r_out=r)
        smooth_step(me, d[2], r, span, d[3], *FACTORS[1], r_out=r)
        al, be = FACTORS[2]

        def extra(x, a, dd, new):
            s = slice(a, a + 8)
            total = (me["x"][x, :, s, :] + d[0][x, :, s, :]) + (d[1][x, :, s, :] + d[2][x, :, s, :])
            me["x"][x, :, s, :] = (total + dd) + (al * dd + be * new)

        smooth_step(me, d[3], r, span, extra=extra)

    l3, l4, l5 = lev[3], lev[4], lev[5]
    whole_pre(3, 2, 16)
    whole_residual(3, 2, 16, l3["d"][0])

    def down_pairs(src, target):
        mid = l3["mid"]

        def body(i, carry):
            v = 0.25 * (src[2 + i, 0, pl.ds(8, 32, stride=2), :] + src[2 + i, 0, pl.ds(10, 32, stride=2), :])
            mid[0, pl.ds(pl.multiple_of(32 * i, 8), 32), :] = v + 0.5 * src[2 + i, 0, pl.ds(9, 32, stride=2), :]
            return carry

        lax.fori_loop(0, 16, body, 0)
        total = dot(mid[0, 0:512, :], rz3[0]) + dot(mid[0, 32:544, :], rz3[1])
        for i in range(16):
            target[1 + i, 0, 8:40, :] = total[32 * i : 32 * i + 32]

    def down_whole(src, target):
        mid = l4["mid"]
        restrict_rows(src, l4["tmp"], mid, 8, 16, 1, 8, 48)
        total = dot(mid[0], rz4[0])
        for i in range(8):
            target[1 + i, 0, 8:24, :] = total[16 * i : 16 * i + 16]

    down_pairs(l3["s"], l4["s"])
    down_whole(l4["s"], l5["s"])
    down_pairs(l3["d"][0], l4["f"])
    whole_pre(4, 1, 16)
    whole_residual(4, 1, 16, l4["d"][0])
    down_whole(l4["d"][0], l5["f"])

    whole_pre(5, 1, 8)
    d5, r5 = l5["d"], l5["r"]

    def turn(x, a, dd, new):
        s = slice(a, a + 8)
        l5["x"][x, :, s, :] = ((d5[0][x, :, s, :] + d5[1][x, :, s, :]) + d5[2][x, :, s, :]) + dd

    smooth_step(l5, d5[3], r5, (1, 9), d5[0], 0.0, 1.0 / CENTER, r_out=r5, extra=turn)
    for k in range(2):
        smooth_step(l5, d5[k], r5, (1, 9), d5[k + 1], *FACTORS[k], r_out=r5)
    al, be = FACTORS[2]

    def last(x, a, dd, new):
        s = slice(a, a + 8)
        total = (l5["x"][x, :, s, :] + d5[0][x, :, s, :]) + d5[1][x, :, s, :]
        l5["x"][x, :, s, :] = (total + dd) + (al * dd + be * new)

    smooth_step(l5, d5[2], r5, (1, 9), extra=last)

    up = dot(l5["x"][1:9, 0, 8:24, :].reshape(128, 128), pz4[0])
    for i in range(8):
        l4["ez"][1 + i, 0, 8:24, :] = up[16 * i : 16 * i + 16]
    interleave(l4["ez"], l4["d"][0], 8, 1, 8, 16, 1, 8)
    whole_post(4, 1, 16)

    e4 = l4["x"]
    up = dot(e4[1:17, 0, 8:40, :].reshape(512, 128), pz3[0]) + dot(e4[0:16, 0, 8:40, :].reshape(512, 128), pz3[1])
    for i in range(16):
        l3["ez"][i, 0, 8:40, :] = up[32 * i : 32 * i + 32]

    def rows_up(i, carry):
        a, b = l3["ez"][i, 0, 8:40, :], l3["ez"][i, 0, 7:39, :]
        l3["d"][0][2 + i, 0, pl.ds(9, 32, stride=2), :] = a
        l3["d"][0][2 + i, 0, pl.ds(8, 32, stride=2), :] = 0.5 * (a + b)
        return carry

    lax.fori_loop(0, 16, rows_up, 0)
    whole_post(3, 2, 16)

    def clear_top(l):
        zero_outside(lev[l]["d"][0], B[l], lower=False)

    def correct(l):
        ex_rho[l].wait_recv()
        ex_rho[l].wait_send()
        zero_outside(lev[l]["rho"], B[l])

    win = l3["x"][pl.ds(2 * gx, 5), 0, pl.ds(4 * gy + 4, 24), :].reshape(120, 128)
    for h in range(2):
        up = dot(win, pz2[h])
        for m in range(5):
            lev[2]["ez"][2 * m + h, 0] = up[24 * m : 24 * m + 24]
    interleave(lev[2]["ez"], lev[2]["d"][0], 8, 2, 2, 16, 0, 8)
    clear_top(2)
    correct(2)
    post(2, lambda x, a, v: store_own(lev[2]["e"], x, a, v, 8))

    for l in (1, 0):
        e = lev[l + 1]["e"]
        ex_e = exchange(e, l + 1, 3, 2)
        sends.append(ex_e)
        correct(l)
        ex_e.wait_recv()
        zero_outside(e, B[l + 1], upper=False)
        ez = lev[l]["ez"]
        er = ez.shape[2]
        step = 7 if l == 0 else 13
        for t in range(0, ez.shape[0], step):
            total = None
            for z in range(ZT[l + 1]):
                v = e[1 + t : 1 + t + step, z, 8 : 8 + er, :].reshape(step * er, 128)
                part = dot(v, pz[l][z])
                total = part if total is None else total + part
            for k in range(step):
                for z in range(ZT[l]):
                    ez[t + k, z] = total[er * k : er * k + er, 128 * z : 128 * z + 128]
        interleave(ez, lev[l]["d"][0], B[l + 1] + 4, 1, 2, (24, 16)[l], 0, 8)
        clear_top(l)
        if l:
            post(l, lambda x, a, v: store_own(lev[1]["e"], x, a, v, 16))
        else:
            def emit(x, a, v):
                lev[0]["x"][x - X0, :, a : a + 8, :] = v
            post(0, emit)

    stores = [
        pltpu.make_async_copy(
            lev[0]["x"].at[:, z, pl.ds(Y0, 32), :], out_hbm.at[:, :, pl.ds(128 * z, 128)], load_sem.at[3, z]
        )
        for z in range(4)
    ]
    for c in stores:
        c.start()
    for ex in ex_s + sends + [gather_s, gather_f]:
        ex.wait_send()
    for c in stores:
        c.wait()


def per_device(right_side, absorption):
    scratch = []

    def vmem(*shape):
        scratch.append(pltpu.VMEM(shape, F32))

    for l in range(3):
        b, zt, rows = B[l], ZT[l], ROWS[l]
        for _ in range(3):
            vmem(b + 9, zt, rows, 128)
        vmem(8, zt, 8 * (CH[l] + 2), 128)
        vmem(zt, (256, 64, 16)[l], 128)
        if l:
            vmem(b + 9, zt, 40, 128)
        if l != 1:
            for _ in range(5):
                vmem(b + 9, zt, rows, 128)
            vmem(b, zt, rows, 128)
        if l:
            vmem(*((13, 2, 24, 128), (10, 1, 24, 128))[l - 1])
    for l in range(3, 6):
        planes, rows = ((20, 88), (18, 48), (10, 32))[l - 3]
        vmem(planes, 1, rows, 128)
        vmem(8, 1, (80, 48, 32)[l - 3], 128)
        vmem(1, (544, 128, 8)[l - 3], 128)
        vmem(*((16, 1, 48, 128), (9, 1, 32, 128), (1, 1, 8, 128))[l - 3])
        if l != 4:
            for _ in range(8):
                vmem(planes, 1, rows, 128)
    vmem(2, 1, 8, 128)
    vmem(2, 1, 8, 128)
    for shape in ((4, 128, 256), (2, 128, 512), (2, 128, 128), (1, 128, 256), (2, 128, 128), (2, 128, 128),
                  (2, 128, 128), (2, 128, 128), (1, 128, 128), (1, 128, 128)):
        vmem(*shape)
    dma = pltpu.SemaphoreType.DMA
    scratch += [dma((4, 4)), dma((12, 8)), dma((12, 8)), dma((2, 24)), dma((2, 24))]
    return pl.pallas_call(
        kernel,
        out_shape=jax.ShapeDtypeStruct((32, 32, 512), F32),
        in_specs=[pl.BlockSpec(memory_space=pl.ANY)] * 2,
        out_specs=pl.BlockSpec(memory_space=pl.ANY),
        scratch_shapes=scratch,
        compiler_params=pltpu.CompilerParams(
            collective_id=0, has_side_effects=True, vmem_limit_bytes=63 * 2**20
        ),
        name="vcycle",
    )(right_side, absorption)


def solution(mesh):
    spec = P("gx", "gy", None)
    return jax.shard_map(per_device, mesh=mesh, in_specs=(spec, spec), out_specs=spec, check_vma=False)
```

```python
import jax
import jax.numpy as jnp
from jax import lax
from jax.experimental import pallas as pl
from jax.experimental.pallas import tpu as pltpu
from jax.sharding import PartitionSpec as P

MESH = pl.DeviceIdType.MESH
CENTER = 0.7875
HALF = 0.6125
GX, GY = 8, 16
X0, Y0 = (4, 8, 8), (12, 16, 16)
PLANES = (41, 32, 24)
EDGE = (4, 5)
OUTER = ((0, 0), (3, 2), (4, 3))
B = (32, 16, 8)
ZT = (4, 2, 1)
ROWS = (56, 48, 40)
CH = (5, 4, 3)
DIRS = [(dx, dy) for dx in (-1, 0, 1) for dy in (-1, 0, 1) if dx or dy]
F32 = jnp.float32


def chebyshev_factors():
    out, q = [], HALF / CENTER
    for _ in range(3):
        n = 1.0 / (2.0 * CENTER / HALF - q)
        out.append((n * q, 2.0 * n / HALF))
        q = n
    return out


FACTORS = chebyshev_factors()


def device(dx, dy):
    return (
        lax.rem(lax.axis_index("gx") + (dx + GX), GX),
        lax.rem(lax.axis_index("gy") + (dy + GY), GY),
    )


def dot(a, b):
    return jnp.dot(a, b, precision=lax.Precision.HIGHEST, preferred_element_type=F32)


def spans(way, width, lo, up, start):
    if way == 0:
        return (start, width), (start, width)
    if way > 0:
        return (start + width - lo, lo), (start - lo, lo)
    return (start, up), (start + width, up)


def remote(src, dst, send, recv, to):
    return pltpu.make_async_remote_copy(
        src_ref=src, dst_ref=dst, send_sem=send, recv_sem=recv, device_id=device(*to), device_id_type=MESH
    )


class Exchange:
    def __init__(self, ref, level, depth, send, recv, slot, dirs=DIRS):
        self.copies = []
        lo, up = depth
        for n, (dx, dy) in enumerate(dirs):
            (sx, nx), (tx, _) = spans(dx, B[level], lo, up, X0[level])
            (sy, ny), (ty, _) = spans(dy, B[level], lo, up, Y0[level])
            src = ref.at[pl.ds(sx, nx), :, pl.ds(sy, ny), :]
            dst = ref.at[pl.ds(tx, nx), :, pl.ds(ty, ny), :]
            self.copies.append(remote(src, dst, send.at[slot, n], recv.at[slot, n], (dx, dy)))

    def start(self):
        for c in self.copies:
            c.start()
        return self

    def wait_recv(self):
        for c in self.copies:
            c.wait_recv()

    def wait_send(self):
        for c in self.copies:
            c.wait_send()


def zero_outside(ref, level, lower=True, upper=True):
    gx, gy = lax.axis_index("gx"), lax.axis_index("gy")
    x0, y0, b = X0[level], Y0[level], B[level]

    def clear(cond, planes, rows):
        @pl.when(cond)
        def _():
            view = (pl.ds(*planes), slice(None), pl.ds(*rows), slice(None))
            ref[view] = jnp.zeros((planes[1], ref.shape[1], rows[1], 128), F32)

    above = min(8, PLANES[level] - x0 - b)
    whole_x, whole_y = (0, x0 + b + above), (8, y0 + b)
    if lower:
        clear(gx == 0, (0, x0), whole_y)
        clear(gy == 0, whole_x, (8, y0 - 8))
    if upper:
        clear(gx == GX - 1, (x0 + b, above), whole_y)
        clear(gy == GY - 1, whole_x, (y0 + b, 8 if level else 5))


def lanes_of(shape):
    return lax.broadcasted_iota(jnp.int32, shape, len(shape) - 1)


def edges(shape, width):
    lane = lanes_of(shape) & (width - 1)
    return lane == 0, lane == width - 1


def z_split(u, masks):
    left, right = pltpu.roll(u, 1, axis=2), pltpu.roll(u, 127, axis=2)
    zero = jnp.zeros_like(u[:1])
    if u.shape[0] > 1:
        before = jnp.concatenate([zero, left[:-1]], 0)
        after = jnp.concatenate([right[1:], zero], 0)
    else:
        before = after = zero
    return u + lax.select(masks[0], before, left) + lax.select(masks[1], after, right)


def z_open(u, masks):
    return u + pltpu.roll(u, 1, axis=2) + pltpu.roll(u, 127, axis=2)


def x_plain(p, n):
    out = []
    for k in range(0, n, 2):
        m = p[k + 1] + p[k + 2]
        out.append(p[k] + m)
        if k + 1 < n:
            out.append(m + p[k + 3])
    return out


def x_pairs(p, n):
    w = [pltpu.roll(v, 64, axis=2) for v in p]
    low = lanes_of(p[0].shape) < 64
    return [p[k + 1] + w[k + 1] + lax.select(low, w[k], w[k + 2]) for k in range(n)]


def smooth_step(lev, src, r, x_range, dst=None, al=0.0, be=0.0, r_out=None, extra=None, after=None, count=None):
    gi, tmp = lev["gi"], lev["tmp"]
    rows = 8 * (lev["ch"] + 2)

    def group(x, n):
        p = [src[x - 1 + k, :, 0:rows, :] for k in range(n + 2)]
        for k, s in enumerate(lev["xsum"](p, n)):
            tmp[k] = s
        h = lev["tall"]
        masks = edges((tmp.shape[1], h, 128), lev["width"])
        for k in range(n):
            for a in range(8, 8 + 8 * lev["ch"], h):
                s = slice(a, a + h)
                u = tmp[k, :, a - 1 : a + h - 1, :] + tmp[k, :, s, :] + tmp[k, :, a + 1 : a + h + 1, :]
                box = lev["zsum"](u, masks)
                d = src[x + k, :, s, :]
                new = (r[x + k, :, s, :] - d) + gi[x + k, :, s, :] * (box - d)
                if extra is not None:
                    extra(x + k, a, d, new)
                if r_out is not None:
                    r_out[x + k, :, s, :] = new
                if dst is not None:
                    dst[x + k, :, s, :] = al * d + be * new

    first, last = x_range
    size = tmp.shape[0]
    if count is not None:
        group(first, count)
        return
    full = (last - first) // size
    rest = (last - first) - full * size
    if full == 1 and after is None:
        group(first, size)
    elif full:
        def body(i, carry):
            group(first + i * size, size)
            if after is not None:
                after(i, first + i * size)
            return carry
        lax.fori_loop(0, full, body, 0)
    if rest:
        group(first + full * size, rest)


def begin(lev, first, count, chunks, mask):
    gi, r, d, f, s = lev["gi"], lev["r"], lev["d"][0], lev["f"], lev["s"]

    def body(i, carry):
        x = first + i
        rows = slice(8, 8 + 8 * chunks)
        g = mask(1.0 / (26.0 + s[x, :, rows, :]), x)
        gi[x, :, rows, :] = g
        new = f[x, :, rows, :] * g
        r[x, :, rows, :] = new
        d[x, :, rows, :] = new * (1.0 / CENTER)
        return carry

    lax.fori_loop(0, count, body, 0)


def store_own(ref, x, a, value, level):
    lo, hi = max(a, Y0[level]), min(a + value.shape[1], Y0[level] + B[level])
    if lo < hi:
        ref[x, :, lo:hi, :] = value[:, lo - a : hi - a, :]


def restrict_rows(src, tmp, out, count, cy, first_plane, first_row, rows):
    size = min(4, count)

    def body(i, carry):
        for k in range(size):
            x = first_plane + 2 * (i * size + k)
            tmp[k] = 0.25 * (src[x, :, 0:rows, :] + src[x + 2, :, 0:rows, :]) + 0.5 * src[x + 1, :, 0:rows, :]
        for k in range(size):
            for z in range(src.shape[1]):
                v = 0.25 * (
                    tmp[k, z, pl.ds(first_row, cy, stride=2), :]
                    + tmp[k, z, pl.ds(first_row + 2, cy, stride=2), :]
                ) + 0.5 * tmp[k, z, pl.ds(first_row + 1, cy, stride=2), :]
                at = (i * size + k) * cy
                if cy % 8 == 0:
                    at = pl.multiple_of(at, 8)
                out[z, pl.ds(at, cy), :] = v
        return carry

    lax.fori_loop(0, count // size, body, 0)


def split_restrict(level, src, tmp, mid, matrix, target):
    cb = B[level + 1]
    x1, y1 = X0[level + 1], Y0[level + 1]
    restrict_rows(src, tmp, mid, cb, cb, X0[level], Y0[level], 8 * (CH[level] + 2))
    total = None
    for z in range(ZT[level]):
        part = dot(mid[z], matrix[z])
        total = part if total is None else total + part
    for i in range(cb):
        for z in range(ZT[level + 1]):
            target[x1 + i, z, y1 : y1 + cb, :] = total[i * cb : (i + 1) * cb, 128 * z : 128 * z + 128]


def interleave(ez, target, count, t0, rows, nj, first_plane, first_row):
    for_z = range(target.shape[1])

    def body(i, carry):
        t = t0 + i
        for z in for_z:
            a1, b1 = ez[t, z, rows : rows + nj, :], ez[t, z, rows - 1 : rows - 1 + nj, :]
            a0, b0 = ez[t - 1, z, rows : rows + nj, :], ez[t - 1, z, rows - 1 : rows - 1 + nj, :]
            odd, even = a1, 0.5 * (a1 + b1)
            odd_0, even_0 = a0, 0.5 * (a0 + b0)
            x = first_plane + 2 * i
            target[x, z, pl.ds(first_row + 1, nj, stride=2), :] = 0.5 * (odd_0 + odd)
            target[x, z, pl.ds(first_row, nj, stride=2), :] = 0.5 * (even_0 + even)
            target[x + 1, z, pl.ds(first_row + 1, nj, stride=2), :] = odd
            target[x + 1, z, pl.ds(first_row, nj, stride=2), :] = even
        return carry

    lax.fori_loop(0, count, body, 0)


def kernel(f_hbm, s_hbm, out_hbm, *refs):
    it = iter(refs)
    lev = []
    for l in range(3):
        me = dict(ch=CH[l], xsum=x_plain, zsum=z_split, tall=(8, 32, 24)[l], width=128)
        for name in ("r", "s", "rho", "tmp", "mid"):
            me[name] = next(it)
        if l == 0:
            me["d"] = [next(it) for _ in range(4)]
            me["gi"], me["f"] = next(it), next(it)
            me["x"] = me["d"][0]
            me["ez"] = me["r"].at[pl.ds(0, 21), :, pl.ds(0, 24), :]
        else:
            old = lev[0]["d"]
            if l == 1:
                views = [old[n].at[pl.ds(0, 32), pl.ds(z, 2), pl.ds(0, 48), :] for n in (2, 3) for z in (0, 2)]
                me["gi"] = old[1].at[pl.ds(0, 32), pl.ds(0, 2), pl.ds(0, 48), :]
            else:
                views = [lev[0]["f"].at[pl.ds(0, 24), pl.ds(z, 1), pl.ds(0, 40), :] for z in range(4)]
                me["gi"] = old[1].at[pl.ds(0, 24), pl.ds(2, 1), pl.ds(0, 40), :]
            me["d"], me["f"] = views, me["r"]
            me["x"], me["ez"] = next(it), next(it)
        lev.append(me)
    for l in range(3, 6):
        me = dict(ch=(8, 4, 2)[l - 3], tall=(32, 32, 16)[l - 3], width=64)
        me["xsum"], me["zsum"] = (x_pairs, z_split) if l == 3 else (x_plain, z_open)
        for name in ("tmp", "mid"):
            me[name] = next(it)
        old = lev[0]["s"]
        if l == 3:
            me["gi"], me["x"] = next(it), next(it)
        elif l == 4:
            me["gi"], me["x"] = [old.at[pl.ds(20, 18), pl.ds(z, 1), pl.ds(0, 48), :] for z in (0, 1)]
        else:
            me["gi"], me["x"], r5, s5 = [old.at[pl.ds(0, 10), pl.ds(z, 1), pl.ds(0, 32), :] for z in range(4)]
            f5 = old.at[pl.ds(10, 10), pl.ds(0, 1), pl.ds(0, 32), :]
        me["ez"] = lev[0]["d"][1].at[pl.ds(0, 16), pl.ds(3, 1), pl.ds(0, 48), :] if l == 3 else next(it)
        if l == 3:
            fields = [next(it) for _ in range(7)]
        elif l == 4:
            old = lev[0]["r"]
            fields = [old.at[pl.ds(x, 18), pl.ds(z, 1), pl.ds(0, 48), :] for x in (0, 18) for z in range(4)][:7]
        else:
            old = lev[0]["f"]
            fields = [old.at[pl.ds(24, 10), pl.ds(z, 1), pl.ds(0, 32), :] for z in range(4)]
            fields += [r5, s5, f5]
        me["d"] = fields[:4]
        me["r"], me["s"], me["f"] = fields[4:]
        lev.append(me)
    blk_f, blk_s = next(it), next(it)
    rz0, pz0, rz1, pz1, rz2, pz2, rz3, pz3, rz4, pz4 = [next(it) for _ in range(10)]
    load_sem, send, recv, wsend, wrecv, gsend, grecv = [next(it) for _ in range(7)]
    gx, gy = lax.axis_index("gx"), lax.axis_index("gy")
    l0, l3, l4, l5 = lev[0], lev[3], lev[4], lev[5]

    loads = []
    for n, (hbm, ref) in enumerate(((s_hbm, l0["s"]), (f_hbm, l0["f"]))):
        for z in range(4):
            c = pltpu.make_async_copy(
                hbm.at[:, :, pl.ds(128 * z, 128)],
                ref.at[pl.ds(X0[0], 32), z, pl.ds(Y0[0], 32), :],
                load_sem.at[n, z],
            )
            c.start()
            loads.append(c)

    def clear_around(ref, off, top):
        n, _, rows, _ = ref.shape
        ref[0:off] = jnp.zeros((off, 1, rows, 128), F32)
        ref[n - off : n] = jnp.zeros((off, 1, rows, 128), F32)
        ref[:, :, 0:8, :] = jnp.zeros((n, 1, 8, 128), F32)
        ref[:, :, top:rows, :] = jnp.zeros((n, 1, rows - top, 128), F32)

    def clear_pads(l):
        me = lev[l]
        top = 8 + 8 * me["ch"]
        for ref in me["d"] + [me["s"]]:
            clear_around(ref, 1, top)
        clear_around(me["x"], 3 if l == 3 else 1, top)
        if l > 3:
            me["ez"][...] = jnp.zeros(me["ez"].shape, F32)
        me["mid"][...] = jnp.zeros(me["mid"].shape, F32)

    clear_pads(3)

    barrier = pltpu.get_barrier_semaphore()
    peers = list(DIRS) + [(d, 0) for d in range(2, GX - 1)] + [(0, d) for d in range(2, GY - 1)]
    for dx, dy in peers:
        pl.semaphore_signal(barrier, inc=1, device_id=device(dx, dy), device_id_type=MESH)
    pl.semaphore_wait(barrier, len(peers))

    slot = iter(range(16))
    rest = []

    def exchange(ref, l, depth, dirs=DIRS):
        return Exchange(ref, l, depth, send, recv, next(slot), dirs).start()

    def piece(c):
        lo, up = EDGE
        x = pl.ds(X0[0] + 8 * c, 8)
        out = []
        for n, ref in enumerate((l0["s"], l0["f"])):
            for m, dy in enumerate((-1, 1)):
                (sy, ny), (ty, _) = spans(dy, 32, lo, up, Y0[0])
                out.append(
                    remote(ref.at[x, :, pl.ds(sy, ny), :], ref.at[x, :, pl.ds(ty, ny), :],
                           wsend.at[c, 2 * n + m], wrecv.at[c, 2 * n + m], (0, dy))
                )
        return out

    for c in loads:
        c.wait()
    for c in piece(0):
        c.start()
    x_dirs = [d for d in DIRS if d[0]]
    ex_x = [exchange(l0["s"], 0, EDGE, x_dirs), exchange(l0["f"], 0, EDGE, x_dirs)]
    for n in range(1, 4):
        for c in piece(n):
            c.start()

    def fill(ref, index, fn):
        shape = ref.shape[1:]
        ref[index] = fn(lax.broadcasted_iota(jnp.int32, shape, 0), lax.broadcasted_iota(jnp.int32, shape, 1))

    def wr(z, k):
        return jnp.where(z == 2 * k + 1, 2.0, jnp.where((z == 2 * k) | (z == 2 * k + 2), 1.0, 0.0))

    def wp(k, z):
        return jnp.where(z == 2 * k + 1, 1.0, jnp.where((z == 2 * k) | (z == 2 * k + 2), 0.5, 0.0))

    for t in range(4):
        fill(rz0, t, lambda z, k: wr(z + 128 * t, k))
    for t in range(2):
        fill(pz0, t, lambda k, z: wp(k + 128 * t, z))
        fill(rz1, t, lambda z, k: wr(z + 128 * t, k))
    fill(pz1, 0, wp)
    for h in range(2):
        fill(rz2, h, lambda z, k: jnp.where((k >> 6) == h, wr(z, k & 63), 0.0))
        fill(pz2, h, lambda k, z: jnp.where((k >> 6) == h, wp(k & 63, z), 0.0))
    fill(rz3, 0, lambda z, k: jnp.where(k < 32, wr(z & 63, k) * jnp.where(z < 64, 0.25, 0.5), 0.0))
    fill(rz3, 1, lambda z, k: jnp.where((k < 32) & (z < 64), wr(z, k) * 0.25, 0.0))
    fill(pz3, 0, lambda k, z: jnp.where(k < 32, wp(k, z & 63) * jnp.where(z < 64, 0.5, 1.0), 0.0))
    fill(pz3, 1, lambda k, z: jnp.where((k < 32) & (z < 64), wp(k, z) * 0.5, 0.0))
    fill(rz4, 0, lambda z, k: jnp.where((k < 16) & (z < 32), wr(z, k), 0.0))
    fill(pz4, 0, lambda k, z: jnp.where((k < 16) & (z < 32), wp(k, z), 0.0))
    rz, pz = (rz0, rz1), (pz0, pz1)

    def pack_block(src, blk):
        mid = lev[2]["mid"]
        restrict_rows(src, lev[2]["tmp"], mid, 4, 4, X0[2], Y0[2], 40)
        lo, hi = dot(mid[0], rz2[0]), dot(mid[0], rz2[1])
        for i in range(2):
            blk[i, 0, 0:4, :] = lo[8 * i : 8 * i + 4] + hi[8 * i + 4 : 8 * i + 8]

    class Gather:
        def __init__(self, n, blk, ref):
            own = ref.at[pl.ds(1 + 2 * gx, 2), :, pl.ds(8 + 4 * gy, 4), :]
            src = blk.at[:, :, pl.ds(0, 4), :]
            slab = ref.at[pl.ds(1, 16), :, pl.ds(8 + 4 * gy, 4), :]
            self.local = pltpu.make_async_copy(src, own, load_sem.at[2, n])
            self.first = [remote(src, own, gsend.at[n, d], grecv.at[n, d], (d, 0)) for d in range(1, GX)]
            self.second = [
                remote(slab, slab, gsend.at[n, 8 + d], grecv.at[n, 8 + d], (0, d)) for d in range(1, GY)
            ]

        def start(self):
            for c in self.first:
                c.start()
            self.local.start()

        def middle(self):
            self.local.wait()
            for c in self.first:
                c.wait_recv()
            for c in self.second:
                c.start()

        def finish(self):
            for c in self.second:
                c.wait_recv()

        def wait_send(self):
            for c in self.first + self.second:
                c.wait_send()

    gather_s = Gather(0, blk_s, l3["s"])
    gather_f = Gather(1, blk_f, l3["f"])

    def edge_mask(l):
        row_lo = jnp.where(gy == 0, Y0[l], 0)
        row_hi = jnp.where(gy == GY - 1, Y0[l] + B[l], 1000)
        x_lo = jnp.where(gx == 0, X0[l], 0)
        x_hi = jnp.where(gx == GX - 1, X0[l] + B[l], 1000)

        def mask(v, x):
            row = lax.broadcasted_iota(jnp.int32, v.shape, 1) + 8
            inside = (row >= row_lo) & (row < row_hi) & (x >= x_lo) & (x < x_hi)
            return jnp.where(inside, v, 0.0)

        return mask

    def pre_stage(l, k, x_range):
        me, b = lev[l], B[l]
        d, r = me["d"], me["r"]
        lo, hi = x_range[0] + X0[l], x_range[1] + X0[l]
        if k < 3:
            smooth_step(me, d[k], r, (lo, hi), d[k + 1], *FACTORS[k], r_out=r)
            return

        def residual(x, a, _, new):
            s = slice(a, a + new.shape[1])
            r[x, :, s, :] = (26.0 + me["s"][x, :, s, :]) * new

        def extra(x, a, dd, new):
            residual(x, a, dd, new)
            store_own(me["rho"], x, a, new, l)
            s = slice(a, a + new.shape[1])
            total = ((d[0][x, :, s, :] + d[1][x, :, s, :]) + d[2][x, :, s, :]) + dd
            if l:
                store_own(me["x"], x, a, total, l)
            else:
                me["x"][x, :, s, :] = total

        end = X0[l] + b
        inside = hi if x_range[1] <= b else end
        if inside > lo:
            smooth_step(me, d[3], r, (lo, inside), extra=extra)
        if inside < hi:
            smooth_step(me, d[3], r, (inside, hi), extra=residual)

    def pre(l):
        me, b = lev[l], B[l]
        begin(me, X0[l] - 7, b + 13, me["ch"], edge_mask(l))
        for k in range(4):
            pre_stage(l, k, (min(k - 3, 0), b + 4 - k))

    def post(l, emit, after=None):
        me, b = lev[l], B[l]
        dl = me["d"][1:] + [me["r"]]
        rho = me["rho"]
        lo, up = OUTER[l]

        def span(w):
            return X0[l] - lo - w, X0[l] + b + up + w

        smooth_step(me, dl[0], rho, span(3), dl[1], 0.0, 1.0 / CENTER, r_out=rho)
        smooth_step(me, dl[1], rho, span(2), dl[2], *FACTORS[0], r_out=rho)
        smooth_step(me, dl[2], rho, span(1), dl[3], *FACTORS[1], r_out=rho)
        al, be = FACTORS[2]

        def extra(x, a, dd, new):
            s = slice(a, a + new.shape[1])
            total = (me["x"][x, :, s, :] + dl[0][x, :, s, :]) + (dl[1][x, :, s, :] + dl[2][x, :, s, :])
            emit(x, a, (total + dd) + (al * dd + be * new))

        smooth_step(me, dl[3], rho, span(0), extra=extra, after=after)

    mask0 = edge_mask(0)

    def wave(x, count):
        begin(l0, X0[0] + x, count, 6, mask0)

    for c in piece(0):
        c.wait_recv()
    wave(0, 8)
    for k in range(3):
        pre_stage(0, k, (k + 1, 7 - k))

    def wave_body(n, carry):
        for c in piece(n):
            c.wait_recv()
        x = 8 * n
        wave(x, 8)
        for k in range(4):
            pre_stage_at(k, x - 1 - k)
        return carry

    def pre_stage_at(k, x):
        d, r = l0["d"], l0["r"]
        lo = X0[0] + x
        if k < 3:
            smooth_step(l0, d[k], r, (lo, lo + 8), d[k + 1], *FACTORS[k], r_out=r, count=8)
        else:
            smooth_step(l0, d[3], r, (lo, lo + 8), extra=last_pre, count=8)

    def last_pre(x, a, dd, new):
        d, s = l0["d"], slice(a, a + new.shape[1])
        l0["r"][x, :, s, :] = (26.0 + l0["s"][x, :, s, :]) * new
        store_own(l0["rho"], x, a, new, 0)
        d[0][x, :, s, :] = ((d[0][x, :, s, :] + d[1][x, :, s, :]) + d[2][x, :, s, :]) + dd

    lax.fori_loop(1, 4, wave_body, 0)
    for ex in ex_x:
        ex.wait_recv()
    wave(32, 5)
    for k in range(4):
        pre_stage(0, k, (31 - k, 36 - k))
    wave(-4, 4)
    for k in range(4):
        pre_stage(0, k, (k - 3, k + 1))

    zero_outside(l0["s"], 0)
    split_restrict(0, l0["s"], l0["tmp"], l0["mid"], rz[0], lev[1]["s"])
    ex_s = exchange(lev[1]["s"], 1, (6, 5))
    rest.append(ex_s)
    split_restrict(0, l0["r"], l0["tmp"], l0["mid"], rz[0], lev[1]["r"])
    ex_f = exchange(lev[1]["r"], 1, EDGE)
    ex_rho = [exchange(l0["rho"], 0, (3, 3))]
    ex_iter = [None]
    for ex in ex_x:
        ex.wait_send()
    for n in range(4):
        for c in piece(n):
            c.wait_send()
    clear_pads(4)
    clear_pads(5)
    l3["ez"][:, :, 0:8, :] = jnp.zeros((16, 1, 8, 128), F32)

    ex_s.wait_recv()
    zero_outside(lev[1]["s"], 1)
    split_restrict(1, lev[1]["s"], lev[1]["tmp"], lev[1]["mid"], rz[1], lev[2]["s"])
    ex_s = exchange(lev[2]["s"], 2, (7, 6))
    rest.append(ex_s)
    ex_f.wait_recv()
    ex_f.wait_send()
    pre(1)
    split_restrict(1, lev[1]["r"], lev[1]["tmp"], lev[1]["mid"], rz[1], lev[2]["r"])
    ex_f = exchange(lev[2]["r"], 2, EDGE)
    ex_rho.append(exchange(lev[1]["rho"], 1, (6, 5)))
    ex_iter.append(exchange(lev[1]["x"], 1, (3, 2)))
    ex_s.wait_recv()
    zero_outside(lev[2]["s"], 2)
    pack_block(lev[2]["s"], blk_s)
    gather_s.start()
    ex_f.wait_recv()
    ex_f.wait_send()
    pre(2)
    pack_block(lev[2]["r"], blk_f)
    gather_f.start()
    gather_s.middle()
    ex_rho.append(exchange(lev[2]["rho"], 2, (7, 6)))
    ex_iter.append(exchange(lev[2]["x"], 2, (4, 3)))
    gather_f.middle()
    rest += [gather_s, gather_f]

    def down_pairs(src, target):
        mid = l3["mid"]

        def body(i, carry):
            v = 0.25 * (src[1 + i, 0, pl.ds(8, 32, stride=2), :] + src[1 + i, 0, pl.ds(10, 32, stride=2), :])
            mid[0, pl.ds(pl.multiple_of(32 * i, 8), 32), :] = v + 0.5 * src[1 + i, 0, pl.ds(9, 32, stride=2), :]
            return carry

        lax.fori_loop(0, 16, body, 0)
        total = dot(mid[0, 0:512, :], rz3[0]) + dot(mid[0, 32:544, :], rz3[1])
        for i in range(16):
            target[1 + i, 0, 8:40, :] = total[32 * i : 32 * i + 32]

    def down_whole(src, target):
        mid = l4["mid"]
        restrict_rows(src, l4["tmp"], mid, 8, 16, 1, 8, 48)
        total = dot(mid[0], rz4[0])
        for i in range(8):
            target[1 + i, 0, 8:24, :] = total[16 * i : 16 * i + 16]

    gather_s.finish()
    down_pairs(l3["s"], l4["s"])
    down_whole(l4["s"], l5["s"])
    gather_f.finish()

    def whole_pre(l, planes):
        me = lev[l]
        d, r = me["d"], me["r"]
        lanes = (128, 32, 16)[l - 3]

        def mask(v, x):
            return v if lanes == 128 else jnp.where(lanes_of(v.shape) < lanes, v, 0.0)

        begin(me, 1, planes, me["ch"], mask)
        for k in range(3):
            smooth_step(me, d[k], r, (1, 1 + planes), d[k + 1], *FACTORS[k], r_out=r)

    def whole_residual(l, planes, f):
        me = lev[l]
        d, r = me["d"], me["r"]
        more = 2 if l == 3 else 0

        def extra(x, a, dd, new):
            s = slice(a, a + new.shape[1])
            me["x"][x + more, :, s, :] = ((d[0][x, :, s, :] + d[1][x, :, s, :]) + d[2][x, :, s, :]) + dd
            f[x, :, s, :] = (26.0 + me["s"][x, :, s, :]) * new

        smooth_step(me, d[3], r, (1, 1 + planes), r_out=r, extra=extra)

    def whole_post(l, planes):
        me = lev[l]
        d, r = me["d"], me["r"]
        span = (1, 1 + planes)
        more = 2 if l == 3 else 0
        smooth_step(me, d[0], r, span, d[1], 0.0, 1.0 / CENTER, r_out=r)
        smooth_step(me, d[1], r, span, d[2], *FACTORS[0], r_out=r)
        smooth_step(me, d[2], r, span, d[3], *FACTORS[1], r_out=r)
        al, be = FACTORS[2]

        def extra(x, a, dd, new):
            s = slice(a, a + new.shape[1])
            total = (me["x"][x + more, :, s, :] + d[0][x, :, s, :]) + (d[1][x, :, s, :] + d[2][x, :, s, :])
            me["x"][x + more, :, s, :] = (total + dd) + (al * dd + be * new)

        smooth_step(me, d[3], r, span, extra=extra)

    whole_pre(3, 16)
    whole_residual(3, 16, l3["d"][0])
    down_pairs(l3["d"][0], l4["f"])
    whole_pre(4, 16)
    whole_residual(4, 16, l4["d"][0])
    down_whole(l4["d"][0], l5["f"])

    whole_pre(5, 8)
    d5, r5 = l5["d"], l5["r"]

    def turn(x, a, dd, new):
        s = slice(a, a + new.shape[1])
        l5["x"][x, :, s, :] = ((d5[0][x, :, s, :] + d5[1][x, :, s, :]) + d5[2][x, :, s, :]) + dd

    smooth_step(l5, d5[3], r5, (1, 9), d5[0], 0.0, 1.0 / CENTER, r_out=r5, extra=turn)
    for k in range(2):
        smooth_step(l5, d5[k], r5, (1, 9), d5[k + 1], *FACTORS[k], r_out=r5)
    al, be = FACTORS[2]

    def last(x, a, dd, new):
        s = slice(a, a + new.shape[1])
        total = (l5["x"][x, :, s, :] + d5[0][x, :, s, :]) + d5[1][x, :, s, :]
        l5["x"][x, :, s, :] = (total + dd) + (al * dd + be * new)

    smooth_step(l5, d5[2], r5, (1, 9), extra=last)

    up = dot(l5["x"][1:9, 0, 8:24, :].reshape(128, 128), pz4[0])
    for i in range(8):
        l4["ez"][1 + i, 0, 8:24, :] = up[16 * i : 16 * i + 16]
    interleave(l4["ez"], l4["d"][0], 8, 1, 8, 16, 1, 8)
    whole_post(4, 16)

    e4 = l4["x"]
    up = dot(e4[1:17, 0, 8:40, :].reshape(512, 128), pz3[0]) + dot(e4[0:16, 0, 8:40, :].reshape(512, 128), pz3[1])
    for i in range(16):
        l3["ez"][i, 0, 8:40, :] = up[32 * i : 32 * i + 32]

    def rows_up(i, carry):
        a, b = l3["ez"][i, 0, 8:40, :], l3["ez"][i, 0, 7:39, :]
        l3["d"][0][1 + i, 0, pl.ds(9, 32, stride=2), :] = a
        l3["d"][0][1 + i, 0, pl.ds(8, 32, stride=2), :] = 0.5 * (a + b)
        return carry

    lax.fori_loop(0, 16, rows_up, 0)
    whole_post(3, 16)

    def correct(l, t0, row, nj):
        count = (20, 15, 12)[l]
        interleave(lev[l]["ez"], lev[l]["d"][1], count, t0, row, nj, 0, 8)
        zero_outside(lev[l]["d"][1], l, lower=False)
        ex_rho[l].wait_recv()
        ex_rho[l].wait_send()
        zero_outside(lev[l]["rho"], l)
        if l:
            ex_iter[l].wait_recv()
            ex_iter[l].wait_send()
            zero_outside(lev[l]["x"], l)

    def emit_to(l):
        def emit(x, a, v):
            lev[l]["x"][x, :, a : a + v.shape[1], :] = v
        return emit

    win = l3["x"][pl.ds(2 * gx, 7), 0, pl.ds(4 * gy, 24), :].reshape(168, 128)
    for h in range(2):
        up = dot(win, pz2[h])
        for m in range(7):
            lev[2]["ez"][2 * m + h, 0] = up[24 * m : 24 * m + 24]
    correct(2, 2, 4, 16)
    post(2, emit_to(2))

    def lift(l, first_plane, first_row, planes, rows, step):
        e, ez = lev[l + 1]["x"], lev[l]["ez"]
        for t in range(0, planes, step):
            total = None
            for z in range(ZT[l + 1]):
                v = e[first_plane + t : first_plane + t + step, z, first_row : first_row + rows, :]
                part = dot(v.reshape(step * rows, 128), pz[l][z])
                total = part if total is None else total + part
            for k in range(step):
                for z in range(ZT[l]):
                    ez[t + k, z] = total[rows * k : rows * k + rows, 128 * z : 128 * z + 128]

    lift(1, 3, 8, 16, 24, 16)
    correct(1, 1, 4, 16)
    post(1, emit_to(1))
    lift(0, 5, 13, 21, 24, 7)
    correct(0, 1, 1, 20)

    def store(i, x):
        return [
            pltpu.make_async_copy(
                l0["x"].at[pl.ds(x, 8), z, pl.ds(Y0[0], 32), :],
                out_hbm.at[pl.ds(x - X0[0], 8), :, pl.ds(128 * z, 128)],
                load_sem.at[4 + i, z],
            )
            for z in range(4)
        ]

    def after(i, x):
        for c in store(i, x):
            c.start()

    post(0, emit_to(0), after)
    for ex in rest:
        ex.wait_send()
    for i in range(4):
        for c in store(i, X0[0] + 8 * i):
            c.wait()


def per_device(right_side, absorption):
    scratch = []

    def vmem(*shape):
        scratch.append(pltpu.VMEM(shape, F32))

    for l in range(3):
        planes, zt, rows = PLANES[l], ZT[l], ROWS[l]
        for _ in range(3):
            vmem(planes, zt, rows, 128)
        vmem(8, zt, 8 * (CH[l] + 2), 128)
        vmem(zt, (256, 64, 16)[l], 128)
        if l == 0:
            for _ in range(6):
                vmem(planes, zt, rows, 128)
        else:
            vmem(planes, zt, rows, 128)
            vmem(*((16, 2, 24, 128), (14, 1, 24, 128))[l - 1])
    for l in range(3, 6):
        vmem(8, 1, (80, 48, 32)[l - 3], 128)
        vmem(1, (544, 128, 8)[l - 3], 128)
        if l == 3:
            vmem(18, 1, 80, 128)
            vmem(22, 1, 88, 128)
            for _ in range(7):
                vmem(18, 1, 80, 128)
        else:
            vmem(*((9, 1, 32, 128), (1, 1, 8, 128))[l - 4])
    vmem(2, 1, 8, 128)
    vmem(2, 1, 8, 128)
    for shape in ((4, 128, 256), (2, 128, 512), (2, 128, 128), (1, 128, 256), (2, 128, 128), (2, 128, 128),
                  (2, 128, 128), (2, 128, 128), (1, 128, 128), (1, 128, 128)):
        vmem(*shape)
    dma = pltpu.SemaphoreType.DMA
    scratch += [dma((8, 4)), dma((12, 8)), dma((12, 8)), dma((4, 4)), dma((4, 4)), dma((2, 24)), dma((2, 24))]
    return pl.pallas_call(
        kernel,
        out_shape=jax.ShapeDtypeStruct((32, 32, 512), F32),
        in_specs=[pl.BlockSpec(memory_space=pl.ANY)] * 2,
        out_specs=pl.BlockSpec(memory_space=pl.ANY),
        scratch_shapes=scratch,
        compiler_params=pltpu.CompilerParams(
            collective_id=0, has_side_effects=True, vmem_limit_bytes=63 * 2**20
        ),
        name="vcycle",
    )(right_side, absorption)


def solution(mesh):
    spec = P("gx", "gy", None)
    return jax.shard_map(per_device, mesh=mesh, in_specs=(spec, spec), out_specs=spec, check_vma=False)
```

```python
import jax
import jax.numpy as jnp
from jax import lax
from jax.experimental import pallas as pl
from jax.experimental.pallas import tpu as pltpu
from jax.sharding import PartitionSpec as P

MESH = pl.DeviceIdType.MESH
CENTER = 0.7875
HALF = 0.6125
GX, GY = 8, 16
X0, Y0 = (4, 8, 8), (12, 16, 16)
PLANES = (41, 32, 24)
EDGE = (4, 5)
OUTER = ((0, 0), (3, 2), (4, 3))
B = (32, 16, 8)
ZT = (4, 2, 1)
ROWS = (56, 48, 40)
CH = (5, 4, 3)
DIRS = [(dx, dy) for dx in (-1, 0, 1) for dy in (-1, 0, 1) if dx or dy]
F32 = jnp.float32


def chebyshev_factors():
    out, q = [], HALF / CENTER
    for _ in range(3):
        n = 1.0 / (2.0 * CENTER / HALF - q)
        out.append((n * q, 2.0 * n / HALF))
        q = n
    return out


FACTORS = chebyshev_factors()


def device(dx, dy):
    return (
        lax.rem(lax.axis_index("gx") + (dx + GX), GX),
        lax.rem(lax.axis_index("gy") + (dy + GY), GY),
    )


def dot(a, b):
    total = None
    for part in range(3):
        if part < 2:
            t = a * 65537.0
            top = t - (t - a)
        else:
            top = a
        p = jnp.dot(top, b, preferred_element_type=F32)
        total = p if total is None else total + p
        a = a - top
    return total


def spans(way, width, lo, up, start):
    if way == 0:
        return (start, width), (start, width)
    if way > 0:
        return (start + width - lo, lo), (start - lo, lo)
    return (start, up), (start + width, up)


def remote(src, dst, send, recv, to):
    return pltpu.make_async_remote_copy(
        src_ref=src, dst_ref=dst, send_sem=send, recv_sem=recv, device_id=device(*to), device_id_type=MESH
    )


class Exchange:
    def __init__(self, ref, level, depth, send, recv, slot, dirs=DIRS):
        self.copies = []
        lo, up = depth
        for n, (dx, dy) in enumerate(dirs):
            (sx, nx), (tx, _) = spans(dx, B[level], lo, up, X0[level])
            (sy, ny), (ty, _) = spans(dy, B[level], lo, up, Y0[level])
            src = ref.at[pl.ds(sx, nx), :, pl.ds(sy, ny), :]
            dst = ref.at[pl.ds(tx, nx), :, pl.ds(ty, ny), :]
            self.copies.append(remote(src, dst, send.at[slot, n], recv.at[slot, n], (dx, dy)))

    def start(self):
        for c in self.copies:
            c.start()
        return self

    def wait_recv(self):
        for c in self.copies:
            c.wait_recv()

    def wait_send(self):
        for c in self.copies:
            c.wait_send()


def zero_outside(ref, level, lower=True, upper=True):
    gx, gy = lax.axis_index("gx"), lax.axis_index("gy")
    x0, y0, b = X0[level], Y0[level], B[level]

    def clear(cond, planes, rows):
        @pl.when(cond)
        def _():
            view = (pl.ds(*planes), slice(None), pl.ds(*rows), slice(None))
            ref[view] = jnp.zeros((planes[1], ref.shape[1], rows[1], 128), F32)

    above = min(8, PLANES[level] - x0 - b)
    whole_x, whole_y = (0, x0 + b + above), (8, y0 + b)
    if lower:
        clear(gx == 0, (0, x0), whole_y)
        clear(gy == 0, whole_x, (8, y0 - 8))
    if upper:
        clear(gx == GX - 1, (x0 + b, above), whole_y)
        clear(gy == GY - 1, whole_x, (y0 + b, 8 if level else 5))


def lanes_of(shape):
    return lax.broadcasted_iota(jnp.int32, shape, len(shape) - 1)


def edges(shape, width):
    lane = lanes_of(shape) & (width - 1)
    return lane == 0, lane == width - 1


def z_split(u, masks):
    left, right = pltpu.roll(u, 1, axis=2), pltpu.roll(u, 127, axis=2)
    zero = jnp.zeros_like(u[:1])
    if u.shape[0] > 1:
        before = jnp.concatenate([zero, left[:-1]], 0)
        after = jnp.concatenate([right[1:], zero], 0)
    else:
        before = after = zero
    return u + lax.select(masks[0], before, left) + lax.select(masks[1], after, right)


def z_open(u, masks):
    return u + pltpu.roll(u, 1, axis=2) + pltpu.roll(u, 127, axis=2)


def x_plain(p, n):
    out = []
    for k in range(0, n, 2):
        m = p[k + 1] + p[k + 2]
        out.append(p[k] + m)
        if k + 1 < n:
            out.append(m + p[k + 3])
    return out


def x_pairs(p, n):
    w = [pltpu.roll(v, 64, axis=2) for v in p]
    low = lanes_of(p[0].shape) < 64
    return [p[k + 1] + w[k + 1] + lax.select(low, w[k], w[k + 2]) for k in range(n)]


def smooth_step(lev, src, r, x_range, dst=None, al=0.0, be=0.0, r_out=None, extra=None, after=None, count=None):
    gi, tmp = lev["gi"], lev["tmp"]
    rows = 8 * (lev["ch"] + 2)

    def group(x, n):
        p = [src[x - 1 + k, :, 0:rows, :] for k in range(n + 2)]
        for k, s in enumerate(lev["xsum"](p, n)):
            tmp[k] = s
        h = lev["tall"]
        masks = edges((tmp.shape[1], h, 128), lev["width"])
        for k in range(n):
            for a in range(8, 8 + 8 * lev["ch"], h):
                s = slice(a, a + h)
                u = tmp[k, :, a - 1 : a + h - 1, :] + tmp[k, :, s, :] + tmp[k, :, a + 1 : a + h + 1, :]
                box = lev["zsum"](u, masks)
                d = src[x + k, :, s, :]
                new = (r[x + k, :, s, :] - d) + gi[x + k, :, s, :] * (box - d)
                if extra is not None:
                    extra(x + k, a, d, new)
                if r_out is not None:
                    r_out[x + k, :, s, :] = new
                if dst is not None:
                    dst[x + k, :, s, :] = al * d + be * new

    first, last = x_range
    size = tmp.shape[0]
    if count is not None:
        group(first, count)
        return
    full = (last - first) // size
    rest = (last - first) - full * size
    if full == 1 and after is None:
        group(first, size)
    elif full:
        def body(i, carry):
            group(first + i * size, size)
            if after is not None:
                after(i, first + i * size)
            return carry
        lax.fori_loop(0, full, body, 0)
    if rest:
        group(first + full * size, rest)


def begin(lev, first, count, chunks, mask):
    gi, r, d, f, s = lev["gi"], lev["r"], lev["d"][0], lev["f"], lev["s"]

    def body(i, carry):
        x = first + i
        rows = slice(8, 8 + 8 * chunks)
        g = mask(1.0 / (26.0 + s[x, :, rows, :]), x)
        gi[x, :, rows, :] = g
        new = f[x, :, rows, :] * g
        r[x, :, rows, :] = new
        d[x, :, rows, :] = new * (1.0 / CENTER)
        return carry

    lax.fori_loop(0, count, body, 0)


def store_own(ref, x, a, value, level):
    lo, hi = max(a, Y0[level]), min(a + value.shape[1], Y0[level] + B[level])
    if lo < hi:
        ref[x, :, lo:hi, :] = value[:, lo - a : hi - a, :]


def restrict_rows(src, tmp, out, count, cy, first_plane, first_row, rows):
    size = min(4, count)

    def body(i, carry):
        restrict_group(i, size, src, tmp, out, cy, first_plane, first_row, rows)
        return carry

    lax.fori_loop(0, count // size, body, 0)


def restrict_group(i, size, src, tmp, out, cy, first_plane, first_row, rows):
    for k in range(size):
        x = first_plane + 2 * (i * size + k)
        tmp[k] = 0.25 * (src[x, :, 0:rows, :] + src[x + 2, :, 0:rows, :]) + 0.5 * src[x + 1, :, 0:rows, :]
    for k in range(size):
        for z in range(src.shape[1]):
            v = 0.25 * (
                tmp[k, z, pl.ds(first_row, cy, stride=2), :]
                + tmp[k, z, pl.ds(first_row + 2, cy, stride=2), :]
            ) + 0.5 * tmp[k, z, pl.ds(first_row + 1, cy, stride=2), :]
            at = (i * size + k) * cy
            if cy % 8 == 0:
                at = pl.multiple_of(at, 8)
            out[z, pl.ds(at, cy), :] = v


def split_restrict(level, src, tmp, mid, matrix, target):
    cb = B[level + 1]
    restrict_rows(src, tmp, mid, cb, cb, X0[level], Y0[level], 8 * (CH[level] + 2))
    split_finish(level, mid, matrix, target)


def split_finish(level, mid, matrix, target):
    cb = B[level + 1]
    x1, y1 = X0[level + 1], Y0[level + 1]
    total = None
    for z in range(ZT[level]):
        part = dot(mid[z], matrix[z])
        total = part if total is None else total + part
    for i in range(cb):
        for z in range(ZT[level + 1]):
            target[x1 + i, z, y1 : y1 + cb, :] = total[i * cb : (i + 1) * cb, 128 * z : 128 * z + 128]


def interleave(ez, target, count, t0, rows, nj, first_plane, first_row):
    for_z = range(target.shape[1])

    def body(i, carry):
        t = t0 + i
        for z in for_z:
            a1, b1 = ez[t, z, rows : rows + nj, :], ez[t, z, rows - 1 : rows - 1 + nj, :]
            a0, b0 = ez[t - 1, z, rows : rows + nj, :], ez[t - 1, z, rows - 1 : rows - 1 + nj, :]
            odd, even = a1, 0.5 * (a1 + b1)
            odd_0, even_0 = a0, 0.5 * (a0 + b0)
            x = first_plane + 2 * i
            target[x, z, pl.ds(first_row + 1, nj, stride=2), :] = 0.5 * (odd_0 + odd)
            target[x, z, pl.ds(first_row, nj, stride=2), :] = 0.5 * (even_0 + even)
            target[x + 1, z, pl.ds(first_row + 1, nj, stride=2), :] = odd
            target[x + 1, z, pl.ds(first_row, nj, stride=2), :] = even
        return carry

    lax.fori_loop(0, count, body, 0)


def kernel(f_hbm, s_hbm, out_hbm, *refs):
    it = iter(refs)
    lev = []
    for l in range(3):
        me = dict(ch=CH[l], xsum=x_plain, zsum=z_split, tall=(8, 32, 24)[l], width=128)
        for name in ("r", "s", "rho", "tmp", "mid"):
            me[name] = next(it)
        if l == 0:
            me["d"] = [next(it) for _ in range(4)]
            me["gi"], me["f"] = next(it), next(it)
            me["x"] = me["f"]
            me["ez"] = me["r"].at[pl.ds(0, 21), :, pl.ds(0, 24), :]
        else:
            old = lev[0]["d"]
            if l == 1:
                views = [old[n].at[pl.ds(0, 32), pl.ds(z, 2), pl.ds(0, 48), :] for n in (2, 3) for z in (0, 2)]
                me["gi"] = old[1].at[pl.ds(0, 32), pl.ds(0, 2), pl.ds(0, 48), :]
            else:
                views = [old[0].at[pl.ds(0, 24), pl.ds(z, 1), pl.ds(0, 40), :] for z in range(4)]
                me["gi"] = old[1].at[pl.ds(0, 24), pl.ds(2, 1), pl.ds(0, 40), :]
            me["d"], me["f"] = views, me["r"]
            me["x"], me["ez"] = next(it), next(it)
        lev.append(me)
    for l in range(3, 6):
        me = dict(ch=(8, 4, 2)[l - 3], tall=(32, 32, 16)[l - 3], width=64)
        me["xsum"], me["zsum"] = (x_pairs, z_split) if l == 3 else (x_plain, z_open)
        for name in ("tmp", "mid"):
            me[name] = next(it)
        old = lev[0]["s"]
        if l == 3:
            me["gi"], me["x"] = next(it), next(it)
        elif l == 4:
            me["gi"], me["x"] = [old.at[pl.ds(20, 18), pl.ds(z, 1), pl.ds(0, 48), :] for z in (0, 1)]
        else:
            me["gi"], me["x"], r5, s5 = [old.at[pl.ds(0, 10), pl.ds(z, 1), pl.ds(0, 32), :] for z in range(4)]
            f5 = old.at[pl.ds(10, 10), pl.ds(0, 1), pl.ds(0, 32), :]
        me["ez"] = lev[0]["d"][1].at[pl.ds(0, 16), pl.ds(3, 1), pl.ds(0, 48), :] if l == 3 else next(it)
        if l == 3:
            fields = [next(it) for _ in range(7)]
        elif l == 4:
            old = lev[0]["r"]
            fields = [old.at[pl.ds(x, 18), pl.ds(z, 1), pl.ds(0, 48), :] for x in (0, 18) for z in range(4)][:7]
        else:
            old = lev[0]["d"][0]
            fields = [old.at[pl.ds(24, 10), pl.ds(z, 1), pl.ds(0, 32), :] for z in range(4)]
            fields += [r5, s5, f5]
        me["d"] = fields[:4]
        me["r"], me["s"], me["f"] = fields[4:]
        lev.append(me)
    blk_f, blk_s = next(it), next(it)
    rz0, pz0, rz1, pz1, rz2, pz2, rz3, pz3, rz4, pz4 = [next(it) for _ in range(10)]
    load_sem, send, recv, wsend, wrecv, gsend, grecv, hello = [next(it) for _ in range(8)]
    gx, gy = lax.axis_index("gx"), lax.axis_index("gy")
    l0, l3, l4, l5 = lev[0], lev[3], lev[4], lev[5]

    loads = []
    for n, (hbm, ref) in enumerate(((s_hbm, l0["s"]), (f_hbm, l0["f"]))):
        for z in range(4):
            c = pltpu.make_async_copy(
                hbm.at[:, :, pl.ds(128 * z, 128)],
                ref.at[pl.ds(X0[0], 32), z, pl.ds(Y0[0], 32), :],
                load_sem.at[n, z],
            )
            c.start()
            loads.append(c)

    def clear_around(ref, off, top):
        n, _, rows, _ = ref.shape
        ref[0:off] = jnp.zeros((off, 1, rows, 128), F32)
        ref[n - off : n] = jnp.zeros((off, 1, rows, 128), F32)
        ref[:, :, 0:8, :] = jnp.zeros((n, 1, 8, 128), F32)
        ref[:, :, top:rows, :] = jnp.zeros((n, 1, rows - top, 128), F32)

    def clear_pads(l):
        me = lev[l]
        top = 8 + 8 * me["ch"]
        for ref in me["d"] + [me["s"]]:
            clear_around(ref, 1, top)
        clear_around(me["x"], 3 if l == 3 else 1, top)
        if l > 3:
            me["ez"][...] = jnp.zeros(me["ez"].shape, F32)
        me["mid"][...] = jnp.zeros(me["mid"].shape, F32)

    barrier = pltpu.get_barrier_semaphore()
    for dx, dy in DIRS:
        pl.semaphore_signal(barrier, inc=1, device_id=device(dx, dy), device_id_type=MESH)
    clear_pads(3)
    pl.semaphore_wait(barrier, len(DIRS))

    rounds = (((1, 0), (-1, 0), (0, 1), (0, -1)), ((2, 0), (-2, 0), (0, 2), (0, -2)), ((0, 4), (0, -4)))

    def greet(n):
        for dx, dy in rounds[n]:
            pl.semaphore_signal(hello.at[n], inc=1, device_id=device(dx, dy), device_id_type=MESH)

    def greeted(n):
        pl.semaphore_wait(hello.at[n], len(rounds[n]))

    slot = iter(range(16))
    rest = []

    def exchange(ref, l, depth, dirs=DIRS):
        return Exchange(ref, l, depth, send, recv, next(slot), dirs).start()

    def piece(c):
        x = pl.ds(X0[0] + 8 * c, 8)
        out = []
        for n, (ref, (lo, up)) in enumerate(((l0["s"], (3, 4)), (l0["d"][0], EDGE))):
            for m, dy in enumerate((-1, 1)):
                (sy, ny), (ty, _) = spans(dy, 32, lo, up, Y0[0])
                out.append(
                    remote(ref.at[x, :, pl.ds(sy, ny), :], ref.at[x, :, pl.ds(ty, ny), :],
                           wsend.at[c, 2 * n + m], wrecv.at[c, 2 * n + m], (0, dy))
                )
        return out

    def begin_own(n, carry):
        own = pl.ds(Y0[0], 32)

        def body(i, inner):
            x = X0[0] + 8 * n + i
            g = 1.0 / (26.0 + l0["s"][x, :, own, :])
            new = l0["f"][x, :, own, :] * g
            l0["gi"][x, :, own, :] = g
            l0["r"][x, :, own, :] = new
            l0["d"][0][x, :, own, :] = new * (1.0 / CENTER)
            return inner

        return lax.fori_loop(0, 8, body, carry)

    for c in loads:
        c.wait()
    begin_own(0, 0)
    for c in piece(0):
        c.start()
    greet(0)
    x_dirs = [d for d in DIRS if d[0]]
    lax.fori_loop(1, 4, begin_own, 0)
    ex_x = [exchange(l0["s"], 0, (3, 4), x_dirs), exchange(l0["d"][0], 0, EDGE, x_dirs)]
    for n in range(1, 4):
        for c in piece(n):
            c.start()

    def fill(ref, index, fn):
        shape = ref.shape[1:]
        ref[index] = fn(lax.broadcasted_iota(jnp.int32, shape, 0), lax.broadcasted_iota(jnp.int32, shape, 1))

    def wr(z, k):
        return jnp.where(z == 2 * k + 1, 2.0, jnp.where((z == 2 * k) | (z == 2 * k + 2), 1.0, 0.0))

    def wp(k, z):
        return jnp.where(z == 2 * k + 1, 1.0, jnp.where((z == 2 * k) | (z == 2 * k + 2), 0.5, 0.0))

    for t in range(4):
        fill(rz0, t, lambda z, k: wr(z + 128 * t, k))
    for t in range(2):
        fill(pz0, t, lambda k, z: wp(k + 128 * t, z))
        fill(rz1, t, lambda z, k: wr(z + 128 * t, k))
    fill(pz1, 0, wp)
    for h in range(2):
        fill(rz2, h, lambda z, k: jnp.where((k >> 6) == h, wr(z, k & 63), 0.0))
        fill(pz2, h, lambda k, z: jnp.where((k >> 6) == h, wp(k & 63, z), 0.0))
    fill(rz3, 0, lambda z, k: jnp.where(k < 32, wr(z & 63, k) * jnp.where(z < 64, 0.25, 0.5), 0.0))
    fill(rz3, 1, lambda z, k: jnp.where((k < 32) & (z < 64), wr(z, k) * 0.25, 0.0))
    fill(pz3, 0, lambda k, z: jnp.where(k < 32, wp(k, z & 63) * jnp.where(z < 64, 0.5, 1.0), 0.0))
    fill(pz3, 1, lambda k, z: jnp.where((k < 32) & (z < 64), wp(k, z) * 0.5, 0.0))
    fill(rz4, 0, lambda z, k: jnp.where((k < 16) & (z < 32), wr(z, k), 0.0))
    fill(pz4, 0, lambda k, z: jnp.where((k < 16) & (z < 32), wp(k, z), 0.0))
    rz, pz = (rz0, rz1), (pz0, pz1)

    def pack_block(src, blk):
        mid = lev[2]["mid"]
        restrict_rows(src, lev[2]["tmp"], mid, 4, 4, X0[2], Y0[2], 40)
        lo, hi = dot(mid[0], rz2[0]), dot(mid[0], rz2[1])
        for i in range(2):
            blk[i, 0, 0:4, :] = lo[8 * i : 8 * i + 4] + hi[8 * i + 4 : 8 * i + 8]

    class Gather:
        def __init__(self, n, blk, ref):
            own = ref.at[pl.ds(1 + 2 * gx, 2), :, pl.ds(8 + 4 * gy, 4), :]
            src = blk.at[:, :, pl.ds(0, 4), :]
            slab = ref.at[pl.ds(1, 16), :, pl.ds(8 + 4 * gy, 4), :]
            self.local = pltpu.make_async_copy(src, own, load_sem.at[2, n])
            self.first = [remote(src, own, gsend.at[n, d], grecv.at[n, d], (d, 0)) for d in range(1, GX)]
            self.second = [
                remote(slab, slab, gsend.at[n, 8 + d], grecv.at[n, 8 + d], (0, d)) for d in range(1, GY)
            ]

        def start(self):
            for c in self.first:
                c.start()
            self.local.start()

        def middle(self):
            self.local.wait()
            for c in self.first:
                c.wait_recv()
            for c in self.second:
                c.start()

        def finish(self):
            for c in self.second:
                c.wait_recv()

        def wait_send(self):
            for c in self.first + self.second:
                c.wait_send()

    gather_s = Gather(0, blk_s, l3["s"])
    gather_f = Gather(1, blk_f, l3["f"])

    def edge_mask(l):
        row_lo = jnp.where(gy == 0, Y0[l], 0)
        row_hi = jnp.where(gy == GY - 1, Y0[l] + B[l], 1000)
        x_lo = jnp.where(gx == 0, X0[l], 0)
        x_hi = jnp.where(gx == GX - 1, X0[l] + B[l], 1000)

        def mask(v, x, a=8):
            row = lax.broadcasted_iota(jnp.int32, v.shape, 1) + a
            inside = (row >= row_lo) & (row < row_hi) & (x >= x_lo) & (x < x_hi)
            return jnp.where(inside, v, 0.0)

        return mask

    def pre_stage(l, k, x_range):
        me, b = lev[l], B[l]
        d, r = me["d"], me["r"]
        lo, hi = x_range[0] + X0[l], x_range[1] + X0[l]
        if k < 3:
            smooth_step(me, d[k], r, (lo, hi), d[k + 1], *FACTORS[k], r_out=r)
            return

        def residual(x, a, _, new):
            s = slice(a, a + new.shape[1])
            r[x, :, s, :] = (26.0 + me["s"][x, :, s, :]) * new

        def extra(x, a, dd, new):
            residual(x, a, dd, new)
            store_own(me["rho"], x, a, new, l)
            s = slice(a, a + new.shape[1])
            total = ((d[0][x, :, s, :] + d[1][x, :, s, :]) + d[2][x, :, s, :]) + dd
            if l:
                store_own(me["x"], x, a, total, l)
            else:
                me["x"][x, :, s, :] = total

        end = X0[l] + b
        inside = hi if x_range[1] <= b else end
        if inside > lo:
            smooth_step(me, d[3], r, (lo, inside), extra=extra)
        if inside < hi:
            smooth_step(me, d[3], r, (inside, hi), extra=residual)

    def pre(l):
        me, b = lev[l], B[l]
        begin(me, X0[l] - 7, b + 13, me["ch"], edge_mask(l))
        for k in range(4):
            pre_stage(l, k, (min(k - 3, 0), b + 4 - k))

    def post(l, emit, after=None):
        me, b = lev[l], B[l]
        dl = me["d"][1:] + [me["r"]]
        rho = me["rho"]
        lo, up = OUTER[l]

        def span(w):
            return X0[l] - lo - w, X0[l] + b + up + w

        smooth_step(me, dl[0], rho, span(3), dl[1], 0.0, 1.0 / CENTER, r_out=rho)
        smooth_step(me, dl[1], rho, span(2), dl[2], *FACTORS[0], r_out=rho)
        smooth_step(me, dl[2], rho, span(1), dl[3], *FACTORS[1], r_out=rho)
        al, be = FACTORS[2]

        def extra(x, a, dd, new):
            s = slice(a, a + new.shape[1])
            total = (me["x"][x, :, s, :] + dl[0][x, :, s, :]) + (dl[1][x, :, s, :] + dl[2][x, :, s, :])
            emit(x, a, (total + dd) + (al * dd + be * new))

        smooth_step(me, dl[3], rho, span(0), extra=extra, after=after)

    mask0 = edge_mask(0)

    def wave(x, count, parts=((8, 4), (44, 5))):
        @pl.when(gy == GY - 1)
        def _():
            l0["s"][pl.ds(X0[0] + x, count), :, 44:49, :] = jnp.zeros((count, 4, 5, 128), F32)

        def body(i, carry):
            at = X0[0] + x + i
            for a, h in parts:
                rows = slice(a, a + h)
                l0["gi"][at, :, rows, :] = mask0(1.0 / (26.0 + l0["s"][at, :, rows, :]), at, a)
                new = mask0(l0["d"][0][at, :, rows, :], at, a)
                l0["d"][0][at, :, rows, :] = new
                l0["r"][at, :, rows, :] = new * CENTER
            return carry

        lax.fori_loop(0, count, body, 0)

    for c in piece(0):
        c.wait_recv()
    greeted(0)
    greet(1)
    wave(0, 8)
    for k in range(3):
        pre_stage(0, k, (k + 1, 7 - k))

    def lift_s(i):
        restrict_group(i, 4, l0["s"], l0["tmp"], l0["mid"], 16, X0[0], Y0[0], 56)

    def wave_body(n, carry):
        for c in piece(n):
            c.wait_recv()
        x = 8 * n
        wave(x, 8)
        for k in range(4):
            pre_stage_at(k, x - 1 - k)
        lift_s(n - 1)
        return carry

    def pre_stage_at(k, x):
        d, r = l0["d"], l0["r"]
        lo = X0[0] + x
        if k < 3:
            smooth_step(l0, d[k], r, (lo, lo + 8), d[k + 1], *FACTORS[k], r_out=r, count=8)
        else:
            smooth_step(l0, d[3], r, (lo, lo + 8), extra=last_pre, count=8)

    def last_pre(x, a, dd, new):
        d, s = l0["d"], slice(a, a + new.shape[1])
        l0["r"][x, :, s, :] = (26.0 + l0["s"][x, :, s, :]) * new
        store_own(l0["rho"], x, a, new, 0)
        l0["x"][x, :, s, :] = ((d[0][x, :, s, :] + d[1][x, :, s, :]) + d[2][x, :, s, :]) + dd

    lax.fori_loop(1, 3, wave_body, 0)
    for ex in ex_x:
        ex.wait_recv()
    greeted(1)
    greet(2)
    wave(-4, 4, ((8, 48),))
    for k in range(4):
        pre_stage(0, k, (k - 3, k + 1))
    wave_body(3, 0)
    wave(32, 5, ((8, 48),))
    for k in range(4):
        pre_stage(0, k, (31 - k, 36 - k))

    @pl.when(gx == GX - 1)
    def _():
        l0["s"][X0[0] + 32] = jnp.zeros((4, 56, 128), F32)

    lift_s(3)
    split_finish(0, l0["mid"], rz[0], lev[1]["s"])
    ex_s = exchange(lev[1]["s"], 1, (6, 5))
    rest.append(ex_s)
    split_restrict(0, l0["r"], l0["tmp"], l0["mid"], rz[0], lev[1]["r"])
    ex_f = exchange(lev[1]["r"], 1, EDGE)
    ex_rho = [exchange(l0["rho"], 0, (3, 3))]
    ex_iter = [None]
    for ex in ex_x:
        ex.wait_send()
    for n in range(4):
        for c in piece(n):
            c.wait_send()
    clear_pads(4)
    clear_pads(5)
    l3["ez"][:, :, 0:8, :] = jnp.zeros((16, 1, 8, 128), F32)

    ex_s.wait_recv()
    zero_outside(lev[1]["s"], 1)
    split_restrict(1, lev[1]["s"], lev[1]["tmp"], lev[1]["mid"], rz[1], lev[2]["s"])
    ex_s = exchange(lev[2]["s"], 2, (7, 6))
    rest.append(ex_s)
    ex_f.wait_recv()
    ex_f.wait_send()
    pre(1)
    split_restrict(1, lev[1]["r"], lev[1]["tmp"], lev[1]["mid"], rz[1], lev[2]["r"])
    ex_f = exchange(lev[2]["r"], 2, EDGE)
    ex_rho.append(exchange(lev[1]["rho"], 1, (6, 5)))
    ex_iter.append(exchange(lev[1]["x"], 1, (3, 2)))
    ex_s.wait_recv()
    zero_outside(lev[2]["s"], 2)
    pack_block(lev[2]["s"], blk_s)
    greeted(2)
    gather_s.start()
    ex_f.wait_recv()
    ex_f.wait_send()
    gather_s.middle()
    pre(2)
    pack_block(lev[2]["r"], blk_f)
    gather_f.start()
    ex_rho.append(exchange(lev[2]["rho"], 2, (7, 6)))
    ex_iter.append(exchange(lev[2]["x"], 2, (4, 3)))
    gather_f.middle()
    rest += [gather_s, gather_f]

    def down_pairs(src, target):
        mid = l3["mid"]

        def body(i, carry):
            v = 0.25 * (src[1 + i, 0, pl.ds(8, 32, stride=2), :] + src[1 + i, 0, pl.ds(10, 32, stride=2), :])
            mid[0, pl.ds(pl.multiple_of(32 * i, 8), 32), :] = v + 0.5 * src[1 + i, 0, pl.ds(9, 32, stride=2), :]
            return carry

        lax.fori_loop(0, 16, body, 0)
        total = dot(mid[0, 0:512, :], rz3[0]) + dot(mid[0, 32:544, :], rz3[1])
        for i in range(16):
            target[1 + i, 0, 8:40, :] = total[32 * i : 32 * i + 32]

    def down_whole(src, target):
        mid = l4["mid"]
        restrict_rows(src, l4["tmp"], mid, 8, 16, 1, 8, 48)
        total = dot(mid[0], rz4[0])
        for i in range(8):
            target[1 + i, 0, 8:24, :] = total[16 * i : 16 * i + 16]

    gather_s.finish()
    down_pairs(l3["s"], l4["s"])
    down_whole(l4["s"], l5["s"])
    gather_f.finish()

    def whole_pre(l, planes):
        me = lev[l]
        d, r = me["d"], me["r"]
        lanes = (128, 32, 16)[l - 3]

        def mask(v, x):
            return v if lanes == 128 else jnp.where(lanes_of(v.shape) < lanes, v, 0.0)

        begin(me, 1, planes, me["ch"], mask)
        for k in range(3):
            smooth_step(me, d[k], r, (1, 1 + planes), d[k + 1], *FACTORS[k], r_out=r)

    def whole_residual(l, planes, f):
        me = lev[l]
        d, r = me["d"], me["r"]
        more = 2 if l == 3 else 0

        def extra(x, a, dd, new):
            s = slice(a, a + new.shape[1])
            me["x"][x + more, :, s, :] = ((d[0][x, :, s, :] + d[1][x, :, s, :]) + d[2][x, :, s, :]) + dd
            f[x, :, s, :] = (26.0 + me["s"][x, :, s, :]) * new

        smooth_step(me, d[3], r, (1, 1 + planes), r_out=r, extra=extra)

    def whole_post(l, planes):
        me = lev[l]
        d, r = me["d"], me["r"]
        span = (1, 1 + planes)
        more = 2 if l == 3 else 0
        smooth_step(me, d[0], r, span, d[1], 0.0, 1.0 / CENTER, r_out=r)
        smooth_step(me, d[1], r, span, d[2], *FACTORS[0], r_out=r)
        smooth_step(me, d[2], r, span, d[3], *FACTORS[1], r_out=r)
        al, be = FACTORS[2]

        def extra(x, a, dd, new):
            s = slice(a, a + new.shape[1])
            total = (me["x"][x + more, :, s, :] + d[0][x, :, s, :]) + (d[1][x, :, s, :] + d[2][x, :, s, :])
            me["x"][x + more, :, s, :] = (total + dd) + (al * dd + be * new)

        smooth_step(me, d[3], r, span, extra=extra)

    whole_pre(3, 16)
    whole_residual(3, 16, l3["d"][0])
    down_pairs(l3["d"][0], l4["f"])
    whole_pre(4, 16)
    whole_residual(4, 16, l4["d"][0])
    down_whole(l4["d"][0], l5["f"])

    whole_pre(5, 8)
    d5, r5 = l5["d"], l5["r"]

    def turn(x, a, dd, new):
        s = slice(a, a + new.shape[1])
        l5["x"][x, :, s, :] = ((d5[0][x, :, s, :] + d5[1][x, :, s, :]) + d5[2][x, :, s, :]) + dd

    smooth_step(l5, d5[3], r5, (1, 9), d5[0], 0.0, 1.0 / CENTER, r_out=r5, extra=turn)
    for k in range(2):
        smooth_step(l5, d5[k], r5, (1, 9), d5[k + 1], *FACTORS[k], r_out=r5)
    al, be = FACTORS[2]

    def last(x, a, dd, new):
        s = slice(a, a + new.shape[1])
        total = (l5["x"][x, :, s, :] + d5[0][x, :, s, :]) + d5[1][x, :, s, :]
        l5["x"][x, :, s, :] = (total + dd) + (al * dd + be * new)

    smooth_step(l5, d5[2], r5, (1, 9), extra=last)

    up = dot(l5["x"][1:9, 0, 8:24, :].reshape(128, 128), pz4[0])
    for i in range(8):
        l4["ez"][1 + i, 0, 8:24, :] = up[16 * i : 16 * i + 16]
    interleave(l4["ez"], l4["d"][0], 8, 1, 8, 16, 1, 8)
    whole_post(4, 16)

    e4 = l4["x"]
    up = dot(e4[1:17, 0, 8:40, :].reshape(512, 128), pz3[0]) + dot(e4[0:16, 0, 8:40, :].reshape(512, 128), pz3[1])
    for i in range(16):
        l3["ez"][i, 0, 8:40, :] = up[32 * i : 32 * i + 32]

    def rows_up(i, carry):
        a, b = l3["ez"][i, 0, 8:40, :], l3["ez"][i, 0, 7:39, :]
        l3["d"][0][1 + i, 0, pl.ds(9, 32, stride=2), :] = a
        l3["d"][0][1 + i, 0, pl.ds(8, 32, stride=2), :] = 0.5 * (a + b)
        return carry

    lax.fori_loop(0, 16, rows_up, 0)
    whole_post(3, 16)

    def correct(l, t0, row, nj):
        count = (20, 15, 12)[l]
        interleave(lev[l]["ez"], lev[l]["d"][1], count, t0, row, nj, 0, 8)
        zero_outside(lev[l]["d"][1], l, lower=False)
        ex_rho[l].wait_recv()
        ex_rho[l].wait_send()
        zero_outside(lev[l]["rho"], l)
        if l:
            ex_iter[l].wait_recv()
            ex_iter[l].wait_send()
            zero_outside(lev[l]["x"], l)

    def emit_to(l):
        def emit(x, a, v):
            lev[l]["x"][x, :, a : a + v.shape[1], :] = v
        return emit

    win = l3["x"][pl.ds(2 * gx, 7), 0, pl.ds(4 * gy, 24), :].reshape(168, 128)
    for h in range(2):
        up = dot(win, pz2[h])
        for m in range(7):
            lev[2]["ez"][2 * m + h, 0] = up[24 * m : 24 * m + 24]
    correct(2, 2, 4, 16)
    post(2, emit_to(2))

    def lift(l, first_plane, first_row, planes, rows, step):
        e, ez = lev[l + 1]["x"], lev[l]["ez"]
        for t in range(0, planes, step):
            total = None
            for z in range(ZT[l + 1]):
                v = e[first_plane + t : first_plane + t + step, z, first_row : first_row + rows, :]
                part = dot(v.reshape(step * rows, 128), pz[l][z])
                total = part if total is None else total + part
            for k in range(step):
                for z in range(ZT[l]):
                    ez[t + k, z] = total[rows * k : rows * k + rows, 128 * z : 128 * z + 128]

    lift(1, 3, 8, 16, 24, 16)
    correct(1, 1, 4, 16)
    post(1, emit_to(1))
    lift(0, 5, 13, 21, 24, 7)
    correct(0, 1, 1, 20)

    def store(i, x):
        return [
            pltpu.make_async_copy(
                l0["x"].at[pl.ds(x, 8), z, pl.ds(Y0[0], 32), :],
                out_hbm.at[pl.ds(x - X0[0], 8), :, pl.ds(128 * z, 128)],
                load_sem.at[4 + i, z],
            )
            for z in range(4)
        ]

    def after(i, x):
        for c in store(i, x):
            c.start()

    post(0, emit_to(0), after)
    for ex in rest:
        ex.wait_send()
    for i in range(4):
        for c in store(i, X0[0] + 8 * i):
            c.wait()


def pass_on(src, dst, held, sem):
    parts = [pl.ds(8 * n, 8) for n in range(4)]
    into = [pltpu.make_async_copy(src.at[p], held.at[p], sem.at[0, n]) for n, p in enumerate(parts)]
    out = [pltpu.make_async_copy(held.at[p], dst.at[p], sem.at[1, n]) for n, p in enumerate(parts)]
    for c in into:
        c.start()
    for a, b in zip(into, out):
        a.wait()
        b.start()
    for c in out:
        c.wait()


def per_device(right_side, absorption):
    scratch = []

    def vmem(*shape):
        scratch.append(pltpu.VMEM(shape, F32))

    for l in range(3):
        planes, zt, rows = PLANES[l], ZT[l], ROWS[l]
        for _ in range(3):
            vmem(planes, zt, rows, 128)
        vmem(8, zt, 8 * (CH[l] + 2), 128)
        vmem(zt, (256, 64, 16)[l], 128)
        if l == 0:
            for _ in range(6):
                vmem(planes, zt, rows, 128)
        else:
            vmem(planes, zt, rows, 128)
            vmem(*((16, 2, 24, 128), (14, 1, 24, 128))[l - 1])
    for l in range(3, 6):
        vmem(8, 1, (80, 48, 32)[l - 3], 128)
        vmem(1, (544, 128, 8)[l - 3], 128)
        if l == 3:
            vmem(18, 1, 80, 128)
            vmem(22, 1, 88, 128)
            for _ in range(7):
                vmem(18, 1, 80, 128)
        else:
            vmem(*((9, 1, 32, 128), (1, 1, 8, 128))[l - 4])
    vmem(2, 1, 8, 128)
    vmem(2, 1, 8, 128)
    for shape in ((4, 128, 256), (2, 128, 512), (2, 128, 128), (1, 128, 256), (2, 128, 128), (2, 128, 128),
                  (2, 128, 128), (2, 128, 128), (1, 128, 128), (1, 128, 128)):
        vmem(*shape)
    dma = pltpu.SemaphoreType.DMA
    scratch += [dma((8, 4)), dma((12, 8)), dma((12, 8)), dma((4, 4)), dma((4, 4)), dma((2, 24)), dma((2, 24)), pltpu.SemaphoreType.REGULAR((3,))]
    result = pl.pallas_call(
        kernel,
        out_shape=jax.ShapeDtypeStruct((32, 32, 512), F32),
        in_specs=[pl.BlockSpec(memory_space=pl.ANY)] * 2,
        out_specs=pl.BlockSpec(memory_space=pl.ANY),
        scratch_shapes=scratch,
        compiler_params=pltpu.CompilerParams(
            collective_id=0, has_side_effects=True, vmem_limit_bytes=63 * 2**20
        ),
        name="vcycle",
    )(right_side, absorption)
    return pl.pallas_call(
        pass_on,
        out_shape=jax.ShapeDtypeStruct((32, 32, 512), F32),
        in_specs=[pl.BlockSpec(memory_space=pl.ANY)],
        out_specs=pl.BlockSpec(memory_space=pl.ANY),
        scratch_shapes=[pltpu.VMEM((32, 32, 512), F32), dma((2, 4))],
        name="pass_on",
    )(result)


def solution(mesh):
    spec = P("gx", "gy", None)
    return jax.shard_map(per_device, mesh=mesh, in_specs=(spec, spec), out_specs=spec, check_vma=False)
```

```python
import jax
import jax.numpy as jnp
from jax import lax
from jax.experimental import pallas as pl
from jax.experimental.pallas import tpu as pltpu
from jax.sharding import PartitionSpec as P

MESH = pl.DeviceIdType.MESH
CENTER = 0.7875
HALF = 0.6125
GX, GY = 8, 16
X0, Y0 = (4, 8, 8), (12, 16, 16)
PLANES = (41, 32, 24)
EDGE = (4, 5)
OUTER = ((0, 0), (3, 2), (4, 3))
B = (32, 16, 8)
ZT = (4, 2, 1)
ROWS = (56, 48, 40)
CH = (5, 4, 3)
DIRS = [(dx, dy) for dx in (-1, 0, 1) for dy in (-1, 0, 1) if dx or dy]
F32 = jnp.float32


def chebyshev_factors():
    out, q = [], HALF / CENTER
    for _ in range(3):
        n = 1.0 / (2.0 * CENTER / HALF - q)
        out.append((n * q, 2.0 * n / HALF))
        q = n
    return out


FACTORS = chebyshev_factors()


def device(dx, dy):
    return (
        lax.rem(lax.axis_index("gx") + (dx + GX), GX),
        lax.rem(lax.axis_index("gy") + (dy + GY), GY),
    )


def dot(a, b):
    total = None
    for part in range(3):
        if part < 2:
            t = a * 65537.0
            top = t - (t - a)
        else:
            top = a
        p = jnp.dot(top, b, preferred_element_type=F32)
        total = p if total is None else total + p
        a = a - top
    return total


def spans(way, width, lo, up, start):
    if way == 0:
        return (start, width), (start, width)
    if way > 0:
        return (start + width - lo, lo), (start - lo, lo)
    return (start, up), (start + width, up)


def remote(src, dst, send, recv, to):
    return pltpu.make_async_remote_copy(
        src_ref=src, dst_ref=dst, send_sem=send, recv_sem=recv, device_id=device(*to), device_id_type=MESH
    )


class Exchange:
    def __init__(self, ref, level, depth, send, recv, slot, dirs=DIRS):
        self.copies = []
        lo, up = depth
        for n, (dx, dy) in enumerate(dirs):
            (sx, nx), (tx, _) = spans(dx, B[level], lo, up, X0[level])
            (sy, ny), (ty, _) = spans(dy, B[level], lo, up, Y0[level])
            src = ref.at[pl.ds(sx, nx), :, pl.ds(sy, ny), :]
            dst = ref.at[pl.ds(tx, nx), :, pl.ds(ty, ny), :]
            self.copies.append(remote(src, dst, send.at[slot, n], recv.at[slot, n], (dx, dy)))

    def start(self):
        for c in self.copies:
            c.start()
        return self

    def wait_recv(self):
        for c in self.copies:
            c.wait_recv()

    def wait_send(self):
        for c in self.copies:
            c.wait_send()


def zero_outside(ref, level, lower=True, upper=True):
    gx, gy = lax.axis_index("gx"), lax.axis_index("gy")
    x0, y0, b = X0[level], Y0[level], B[level]

    def clear(cond, planes, rows):
        @pl.when(cond)
        def _():
            view = (pl.ds(*planes), slice(None), pl.ds(*rows), slice(None))
            ref[view] = jnp.zeros((planes[1], ref.shape[1], rows[1], 128), F32)

    above = min(8, PLANES[level] - x0 - b)
    whole_x, whole_y = (0, x0 + b + above), (8, y0 + b)
    if lower:
        clear(gx == 0, (0, x0), whole_y)
        clear(gy == 0, whole_x, (8, y0 - 8))
    if upper:
        clear(gx == GX - 1, (x0 + b, above), whole_y)
        clear(gy == GY - 1, whole_x, (y0 + b, 8 if level else 5))


def lanes_of(shape):
    return lax.broadcasted_iota(jnp.int32, shape, len(shape) - 1)


def edges(shape, width):
    lane = lanes_of(shape) & (width - 1)
    return lane == 0, lane == width - 1


def z_split(u, masks):
    left, right = pltpu.roll(u, 1, axis=2), pltpu.roll(u, 127, axis=2)
    zero = jnp.zeros_like(u[:1])
    if u.shape[0] > 1:
        before = jnp.concatenate([zero, left[:-1]], 0)
        after = jnp.concatenate([right[1:], zero], 0)
    else:
        before = after = zero
    return u + lax.select(masks[0], before, left) + lax.select(masks[1], after, right)


def z_open(u, masks):
    return u + pltpu.roll(u, 1, axis=2) + pltpu.roll(u, 127, axis=2)


def x_plain(p, n):
    out = []
    for k in range(0, n, 2):
        m = p[k + 1] + p[k + 2]
        out.append(p[k] + m)
        if k + 1 < n:
            out.append(m + p[k + 3])
    return out


def x_pairs(p, n):
    w = [pltpu.roll(v, 64, axis=2) for v in p]
    low = lanes_of(p[0].shape) < 64
    return [p[k + 1] + w[k + 1] + lax.select(low, w[k], w[k + 2]) for k in range(n)]


def smooth_step(lev, src, r, x_range, dst=None, al=0.0, be=0.0, r_out=None, extra=None, after=None, count=None):
    gi, tmp = lev["gi"], lev["tmp"]
    rows = 8 * (lev["ch"] + 2)

    def group(x, n):
        p = [src[x - 1 + k, :, 0:rows, :] for k in range(n + 2)]
        for k, s in enumerate(lev["xsum"](p, n)):
            tmp[k] = s
        h = lev["tall"]
        masks = edges((tmp.shape[1], h, 128), lev["width"])
        for k in range(n):
            for a in range(8, 8 + 8 * lev["ch"], h):
                s = slice(a, a + h)
                u = tmp[k, :, a - 1 : a + h - 1, :] + tmp[k, :, s, :] + tmp[k, :, a + 1 : a + h + 1, :]
                box = lev["zsum"](u, masks)
                d = src[x + k, :, s, :]
                new = (r[x + k, :, s, :] - d) + gi[x + k, :, s, :] * (box - d)
                if extra is not None:
                    extra(x + k, a, d, new)
                if r_out is not None:
                    r_out[x + k, :, s, :] = new
                if dst is not None:
                    dst[x + k, :, s, :] = al * d + be * new

    first, last = x_range
    size = tmp.shape[0]
    if count is not None:
        group(first, count)
        return
    full = (last - first) // size
    rest = (last - first) - full * size
    if full == 1 and after is None:
        group(first, size)
    elif full:
        def body(i, carry):
            group(first + i * size, size)
            if after is not None:
                after(i, first + i * size)
            return carry
        lax.fori_loop(0, full, body, 0)
    if rest:
        group(first + full * size, rest)


def begin_gi(lev, first, count, chunks, mask):
    gi, s = lev["gi"], lev["s"]

    def body(i, carry):
        x = first + i
        rows = slice(8, 8 + 8 * chunks)
        gi[x, :, rows, :] = mask(1.0 / (26.0 + s[x, :, rows, :]), x)
        return carry

    lax.fori_loop(0, count, body, 0)


def begin(lev, first, count, chunks):
    gi, r, d, f = lev["gi"], lev["r"], lev["d"][0], lev["f"]

    def body(i, carry):
        x = first + i
        rows = slice(8, 8 + 8 * chunks)
        new = f[x, :, rows, :] * gi[x, :, rows, :]
        r[x, :, rows, :] = new
        d[x, :, rows, :] = new * (1.0 / CENTER)
        return carry

    lax.fori_loop(0, count, body, 0)


def store_own(ref, x, a, value, level):
    lo, hi = max(a, Y0[level]), min(a + value.shape[1], Y0[level] + B[level])
    if lo < hi:
        ref[x, :, lo:hi, :] = value[:, lo - a : hi - a, :]


def restrict_rows(src, tmp, out, count, cy, first_plane, first_row, rows):
    size = min(4, count)

    def body(i, carry):
        restrict_group(i, size, src, tmp, out, cy, first_plane, first_row, rows)
        return carry

    lax.fori_loop(0, count // size, body, 0)


def restrict_group(i, size, src, tmp, out, cy, first_plane, first_row, rows):
    for k in range(size):
        x = first_plane + 2 * (i * size + k)
        tmp[k] = 0.25 * (src[x, :, 0:rows, :] + src[x + 2, :, 0:rows, :]) + 0.5 * src[x + 1, :, 0:rows, :]
    for k in range(size):
        for z in range(src.shape[1]):
            v = 0.25 * (
                tmp[k, z, pl.ds(first_row, cy, stride=2), :]
                + tmp[k, z, pl.ds(first_row + 2, cy, stride=2), :]
            ) + 0.5 * tmp[k, z, pl.ds(first_row + 1, cy, stride=2), :]
            at = (i * size + k) * cy
            if cy % 8 == 0:
                at = pl.multiple_of(at, 8)
            out[z, pl.ds(at, cy), :] = v


def split_restrict(level, src, tmp, mid, matrix, target):
    cb = B[level + 1]
    restrict_rows(src, tmp, mid, cb, cb, X0[level], Y0[level], 8 * (CH[level] + 2))
    split_finish(level, mid, matrix, target)


def split_finish(level, mid, matrix, target):
    cb = B[level + 1]
    x1, y1 = X0[level + 1], Y0[level + 1]
    total = None
    for z in range(ZT[level]):
        part = dot(mid[z], matrix[z])
        total = part if total is None else total + part
    for i in range(cb):
        for z in range(ZT[level + 1]):
            target[x1 + i, z, y1 : y1 + cb, :] = total[i * cb : (i + 1) * cb, 128 * z : 128 * z + 128]


def interleave(ez, target, count, t0, rows, nj, first_plane, first_row):
    for_z = range(target.shape[1])

    def body(i, carry):
        t = t0 + i
        for z in for_z:
            a1, b1 = ez[t, z, rows : rows + nj, :], ez[t, z, rows - 1 : rows - 1 + nj, :]
            a0, b0 = ez[t - 1, z, rows : rows + nj, :], ez[t - 1, z, rows - 1 : rows - 1 + nj, :]
            odd, even = a1, 0.5 * (a1 + b1)
            odd_0, even_0 = a0, 0.5 * (a0 + b0)
            x = first_plane + 2 * i
            target[x, z, pl.ds(first_row + 1, nj, stride=2), :] = 0.5 * (odd_0 + odd)
            target[x, z, pl.ds(first_row, nj, stride=2), :] = 0.5 * (even_0 + even)
            target[x + 1, z, pl.ds(first_row + 1, nj, stride=2), :] = odd
            target[x + 1, z, pl.ds(first_row, nj, stride=2), :] = even
        return carry

    lax.fori_loop(0, count, body, 0)


def kernel(f_hbm, s_hbm, out_hbm, *refs):
    it = iter(refs)
    lev = []
    for l in range(3):
        me = dict(ch=CH[l], xsum=x_plain, zsum=z_split, tall=(8, 32, 24)[l], width=128)
        for name in ("r", "s", "rho", "tmp", "mid"):
            me[name] = next(it)
        if l == 0:
            me["d"] = [next(it) for _ in range(4)]
            me["gi"], me["f"] = next(it), next(it)
            me["x"] = me["f"]
            me["ez"] = me["r"].at[pl.ds(0, 21), :, pl.ds(0, 24), :]
        else:
            old = lev[0]["d"]
            if l == 1:
                views = [old[n].at[pl.ds(0, 32), pl.ds(z, 2), pl.ds(0, 48), :] for n in (2, 3) for z in (0, 2)]
                me["gi"] = old[1].at[pl.ds(0, 32), pl.ds(0, 2), pl.ds(0, 48), :]
            else:
                views = [old[0].at[pl.ds(0, 24), pl.ds(z, 1), pl.ds(0, 40), :] for z in range(4)]
                me["gi"] = old[1].at[pl.ds(0, 24), pl.ds(2, 1), pl.ds(0, 40), :]
            me["d"], me["f"] = views, me["r"]
            me["x"], me["ez"] = next(it), next(it)
        lev.append(me)
    for l in range(3, 6):
        me = dict(ch=(8, 4, 2)[l - 3], tall=(32, 32, 16)[l - 3], width=64)
        me["xsum"], me["zsum"] = (x_pairs, z_split) if l == 3 else (x_plain, z_open)
        old = lev[0]["s"]
        if l == 3:
            me["tmp"] = next(it)
        elif l == 4:
            me["tmp"] = old.at[pl.ds(20, 16), pl.ds(2, 1), pl.ds(0, 48), :]
        else:
            me["tmp"] = old.at[pl.ds(10, 8), pl.ds(1, 1), pl.ds(0, 32), :]
        me["mid"] = next(it)
        if l == 3:
            me["gi"], me["x"] = next(it), next(it)
        elif l == 4:
            me["gi"], me["x"] = [old.at[pl.ds(20, 18), pl.ds(z, 1), pl.ds(0, 48), :] for z in (0, 1)]
        else:
            me["gi"], me["x"], r5, s5 = [old.at[pl.ds(0, 10), pl.ds(z, 1), pl.ds(0, 32), :] for z in range(4)]
            f5 = old.at[pl.ds(10, 10), pl.ds(0, 1), pl.ds(0, 32), :]
        if l == 3:
            me["ez"] = lev[0]["d"][1].at[pl.ds(0, 16), pl.ds(3, 1), pl.ds(0, 48), :]
        else:
            me["ez"] = old.at[pl.ds(10, 9), pl.ds(l - 2, 1), pl.ds(0, 32), :]
        if l == 3:
            fields = [next(it) for _ in range(7)]
        elif l == 4:
            old = lev[0]["r"]
            fields = [old.at[pl.ds(x, 18), pl.ds(z, 1), pl.ds(0, 48), :] for x in (0, 18) for z in range(4)][:7]
        else:
            old = lev[0]["d"][0]
            fields = [old.at[pl.ds(24, 10), pl.ds(z, 1), pl.ds(0, 32), :] for z in range(4)]
            fields += [r5, s5, f5]
        me["d"] = fields[:4]
        me["r"], me["s"], me["f"] = fields[4:]
        lev.append(me)
    blk_f, blk_s = next(it), next(it)
    rz0, pz0, rz1, pz1, rz2, pz2, rz3, pz3, rz4, pz4 = [next(it) for _ in range(10)]
    load_sem, send, recv, wsend, wrecv, gsend, grecv, hello = [next(it) for _ in range(8)]
    gx, gy = lax.axis_index("gx"), lax.axis_index("gy")
    l0, l3, l4, l5 = lev[0], lev[3], lev[4], lev[5]

    loads = []
    for n, (hbm, ref) in enumerate(((s_hbm, l0["s"]), (f_hbm, l0["f"]))):
        for z in range(4):
            c = pltpu.make_async_copy(
                hbm.at[:, :, pl.ds(128 * z, 128)],
                ref.at[pl.ds(X0[0], 32), z, pl.ds(Y0[0], 32), :],
                load_sem.at[n, z],
            )
            c.start()
            loads.append(c)

    def clear_around(ref, off, top):
        n, _, rows, _ = ref.shape
        ref[0:off] = jnp.zeros((off, 1, rows, 128), F32)
        ref[n - off : n] = jnp.zeros((off, 1, rows, 128), F32)
        ref[:, :, 0:8, :] = jnp.zeros((n, 1, 8, 128), F32)
        ref[:, :, top:rows, :] = jnp.zeros((n, 1, rows - top, 128), F32)

    def clear_pads(l):
        me = lev[l]
        top = 8 + 8 * me["ch"]
        for ref in me["d"] + [me["s"]]:
            clear_around(ref, 1, top)
        clear_around(me["x"], 3 if l == 3 else 1, top)
        if l > 3:
            me["ez"][...] = jnp.zeros(me["ez"].shape, F32)
        me["mid"][...] = jnp.zeros(me["mid"].shape, F32)

    barrier = pltpu.get_barrier_semaphore()
    for dx, dy in DIRS:
        pl.semaphore_signal(barrier, inc=1, device_id=device(dx, dy), device_id_type=MESH)
    clear_pads(3)
    pl.semaphore_wait(barrier, len(DIRS))

    rounds = (((1, 0), (-1, 0), (0, 1), (0, -1)), ((2, 0), (-2, 0), (0, 2), (0, -2)), ((0, 4), (0, -4)))

    def greet(n):
        for dx, dy in rounds[n]:
            pl.semaphore_signal(hello.at[n], inc=1, device_id=device(dx, dy), device_id_type=MESH)

    def greeted(n):
        pl.semaphore_wait(hello.at[n], len(rounds[n]))

    slot = iter(range(16))
    rest = []

    def exchange(ref, l, depth, dirs=DIRS):
        return Exchange(ref, l, depth, send, recv, next(slot), dirs).start()

    def piece(c):
        x = pl.ds(X0[0] + 8 * c, 8)
        out = []
        for n, (ref, (lo, up)) in enumerate(((l0["s"], (3, 4)), (l0["d"][0], EDGE))):
            for m, dy in enumerate((-1, 1)):
                (sy, ny), (ty, _) = spans(dy, 32, lo, up, Y0[0])
                out.append(
                    remote(ref.at[x, :, pl.ds(sy, ny), :], ref.at[x, :, pl.ds(ty, ny), :],
                           wsend.at[c, 2 * n + m], wrecv.at[c, 2 * n + m], (0, dy))
                )
        return out

    def begin_own(n, carry):
        own = pl.ds(Y0[0], 32)

        def body(i, inner):
            x = X0[0] + 8 * n + i
            g = 1.0 / (26.0 + l0["s"][x, :, own, :])
            new = l0["f"][x, :, own, :] * g
            l0["gi"][x, :, own, :] = g
            l0["r"][x, :, own, :] = new
            l0["d"][0][x, :, own, :] = new * (1.0 / CENTER)
            return inner

        return lax.fori_loop(0, 8, body, carry)

    for c in loads:
        c.wait()
    begin_own(0, 0)
    for c in piece(0):
        c.start()
    greet(0)
    x_dirs = [d for d in DIRS if d[0]]
    lax.fori_loop(1, 4, begin_own, 0)
    ex_x = [exchange(l0["s"], 0, (3, 4), x_dirs), exchange(l0["d"][0], 0, EDGE, x_dirs)]
    for n in range(1, 4):
        for c in piece(n):
            c.start()

    def fill(ref, index, fn):
        shape = ref.shape[1:]
        ref[index] = fn(lax.broadcasted_iota(jnp.int32, shape, 0), lax.broadcasted_iota(jnp.int32, shape, 1))

    def wr(z, k):
        return jnp.where(z == 2 * k + 1, 2.0, jnp.where((z == 2 * k) | (z == 2 * k + 2), 1.0, 0.0))

    def wp(k, z):
        return jnp.where(z == 2 * k + 1, 1.0, jnp.where((z == 2 * k) | (z == 2 * k + 2), 0.5, 0.0))

    for t in range(4):
        fill(rz0, t, lambda z, k: wr(z + 128 * t, k))
    for t in range(2):
        fill(pz0, t, lambda k, z: wp(k + 128 * t, z))
        fill(rz1, t, lambda z, k: wr(z + 128 * t, k))
    fill(pz1, 0, wp)
    for h in range(2):
        fill(rz2, h, lambda z, k: jnp.where((k >> 6) == h, wr(z, k & 63), 0.0))
        fill(pz2, h, lambda k, z: jnp.where((k >> 6) == h, wp(k & 63, z), 0.0))
    fill(rz3, 0, lambda z, k: jnp.where(k < 32, wr(z & 63, k) * jnp.where(z < 64, 0.25, 0.5), 0.0))
    fill(rz3, 1, lambda z, k: jnp.where((k < 32) & (z < 64), wr(z, k) * 0.25, 0.0))
    fill(pz3, 0, lambda k, z: jnp.where(k < 32, wp(k, z & 63) * jnp.where(z < 64, 0.5, 1.0), 0.0))
    fill(pz3, 1, lambda k, z: jnp.where((k < 32) & (z < 64), wp(k, z) * 0.5, 0.0))
    fill(rz4, 0, lambda z, k: jnp.where((k < 16) & (z < 32), wr(z, k), 0.0))
    fill(pz4, 0, lambda k, z: jnp.where((k < 16) & (z < 32), wp(k, z), 0.0))
    rz, pz = (rz0, rz1), (pz0, pz1)

    def pack_block(src, blk):
        mid = lev[2]["mid"]
        restrict_rows(src, lev[2]["tmp"], mid, 4, 4, X0[2], Y0[2], 40)
        lo, hi = dot(mid[0], rz2[0]), dot(mid[0], rz2[1])
        for i in range(2):
            blk[i, 0, 0:4, :] = lo[8 * i : 8 * i + 4] + hi[8 * i + 4 : 8 * i + 8]

    class Gather:
        def __init__(self, n, blk, ref):
            own = ref.at[pl.ds(1 + 2 * gx, 2), :, pl.ds(8 + 4 * gy, 4), :]
            src = blk.at[:, :, pl.ds(0, 4), :]
            slab = ref.at[pl.ds(1, 16), :, pl.ds(8 + 4 * gy, 4), :]
            self.local = pltpu.make_async_copy(src, own, load_sem.at[2, n])
            self.first = [remote(src, own, gsend.at[n, d], grecv.at[n, d], (d, 0)) for d in range(1, GX)]
            self.second = [
                remote(slab, slab, gsend.at[n, 8 + d], grecv.at[n, 8 + d], (0, d)) for d in range(1, GY)
            ]

        def start(self):
            for c in self.first:
                c.start()
            self.local.start()

        def middle(self):
            self.local.wait()
            for c in self.first:
                c.wait_recv()
            for c in self.second:
                c.start()

        def finish(self):
            for c in self.second:
                c.wait_recv()

        def wait_send(self):
            for c in self.first + self.second:
                c.wait_send()

    gather_s = Gather(0, blk_s, l3["s"])
    gather_f = Gather(1, blk_f, l3["f"])

    def edge_mask(l):
        row_lo = jnp.where(gy == 0, Y0[l], 0)
        row_hi = jnp.where(gy == GY - 1, Y0[l] + B[l], 1000)
        x_lo = jnp.where(gx == 0, X0[l], 0)
        x_hi = jnp.where(gx == GX - 1, X0[l] + B[l], 1000)

        def mask(v, x, a=8):
            row = lax.broadcasted_iota(jnp.int32, v.shape, 1) + a
            inside = (row >= row_lo) & (row < row_hi) & (x >= x_lo) & (x < x_hi)
            return jnp.where(inside, v, 0.0)

        return mask

    def pre_stage(l, k, x_range):
        me, b = lev[l], B[l]
        d, r = me["d"], me["r"]
        lo, hi = x_range[0] + X0[l], x_range[1] + X0[l]
        if k < 3:
            smooth_step(me, d[k], r, (lo, hi), d[k + 1], *FACTORS[k], r_out=r)
            return

        def residual(x, a, _, new):
            s = slice(a, a + new.shape[1])
            r[x, :, s, :] = (26.0 + me["s"][x, :, s, :]) * new

        def extra(x, a, dd, new):
            residual(x, a, dd, new)
            store_own(me["rho"], x, a, new, l)
            s = slice(a, a + new.shape[1])
            total = ((d[0][x, :, s, :] + d[1][x, :, s, :]) + d[2][x, :, s, :]) + dd
            if l:
                store_own(me["x"], x, a, total, l)
            else:
                me["x"][x, :, s, :] = total

        end = X0[l] + b
        inside = hi if x_range[1] <= b else end
        if inside > lo:
            smooth_step(me, d[3], r, (lo, inside), extra=extra)
        if inside < hi:
            smooth_step(me, d[3], r, (inside, hi), extra=residual)

    def pre_gi(l):
        begin_gi(lev[l], X0[l] - 7, B[l] + 13, lev[l]["ch"], edge_mask(l))

    def pre(l):
        me, b = lev[l], B[l]
        begin(me, X0[l] - 4, b + 9, me["ch"])
        for k in range(4):
            pre_stage(l, k, (min(k - 3, 0), b + 4 - k))

    def post(l, emit, after=None):
        me, b = lev[l], B[l]
        dl = me["d"][1:] + [me["r"]]
        rho = me["rho"]
        lo, up = OUTER[l]

        def span(w):
            return X0[l] - lo - w, X0[l] + b + up + w

        smooth_step(me, dl[0], rho, span(3), dl[1], 0.0, 1.0 / CENTER, r_out=rho)
        smooth_step(me, dl[1], rho, span(2), dl[2], *FACTORS[0], r_out=rho)
        smooth_step(me, dl[2], rho, span(1), dl[3], *FACTORS[1], r_out=rho)
        al, be = FACTORS[2]

        def extra(x, a, dd, new):
            s = slice(a, a + new.shape[1])
            total = (me["x"][x, :, s, :] + dl[0][x, :, s, :]) + (dl[1][x, :, s, :] + dl[2][x, :, s, :])
            emit(x, a, (total + dd) + (al * dd + be * new))

        smooth_step(me, dl[3], rho, span(0), extra=extra, after=after)

    mask0 = edge_mask(0)

    def wave(x, count, parts=((8, 4), (44, 5))):
        @pl.when(gy == GY - 1)
        def _():
            l0["s"][pl.ds(X0[0] + x, count), :, 44:49, :] = jnp.zeros((count, 4, 5, 128), F32)

        def body(i, carry):
            at = X0[0] + x + i
            for a, h in parts:
                rows = slice(a, a + h)
                l0["gi"][at, :, rows, :] = mask0(1.0 / (26.0 + l0["s"][at, :, rows, :]), at, a)
                new = mask0(l0["d"][0][at, :, rows, :], at, a)
                l0["d"][0][at, :, rows, :] = new
                l0["r"][at, :, rows, :] = new * CENTER
            return carry

        lax.fori_loop(0, count, body, 0)

    for c in piece(0):
        c.wait_recv()
    greeted(0)
    greet(1)
    wave(0, 8)
    for k in range(3):
        pre_stage(0, k, (k + 1, 7 - k))

    def lift_s(i):
        restrict_group(i, 4, l0["s"], l0["tmp"], l0["mid"], 16, X0[0], Y0[0], 56)

    def wave_body(n, carry):
        for c in piece(n):
            c.wait_recv()
        x = 8 * n
        wave(x, 8)
        for k in range(4):
            pre_stage_at(k, x - 1 - k)
        lift_s(n - 1)
        return carry

    def pre_stage_at(k, x):
        d, r = l0["d"], l0["r"]
        lo = X0[0] + x
        if k < 3:
            smooth_step(l0, d[k], r, (lo, lo + 8), d[k + 1], *FACTORS[k], r_out=r, count=8)
        else:
            smooth_step(l0, d[3], r, (lo, lo + 8), extra=last_pre, count=8)

    def last_pre(x, a, dd, new):
        d, s = l0["d"], slice(a, a + new.shape[1])
        l0["r"][x, :, s, :] = (26.0 + l0["s"][x, :, s, :]) * new
        store_own(l0["rho"], x, a, new, 0)
        l0["x"][x, :, s, :] = ((d[0][x, :, s, :] + d[1][x, :, s, :]) + d[2][x, :, s, :]) + dd

    lax.fori_loop(1, 3, wave_body, 0)
    for ex in ex_x:
        ex.wait_recv()
    greeted(1)
    greet(2)
    wave(-4, 4, ((8, 48),))
    for k in range(4):
        pre_stage(0, k, (k - 3, k + 1))
    wave_body(3, 0)
    wave(32, 5, ((8, 48),))
    for k in range(4):
        pre_stage(0, k, (31 - k, 36 - k))

    @pl.when(gx == GX - 1)
    def _():
        l0["s"][X0[0] + 32] = jnp.zeros((4, 56, 128), F32)

    lift_s(3)
    split_finish(0, l0["mid"], rz[0], lev[1]["s"])
    ex_s = exchange(lev[1]["s"], 1, (6, 5))
    rest.append(ex_s)
    split_restrict(0, l0["r"], l0["tmp"], l0["mid"], rz[0], lev[1]["r"])
    ex_f = exchange(lev[1]["r"], 1, EDGE)
    ex_rho = [exchange(l0["rho"], 0, (3, 3))]
    ex_iter = [None]
    for ex in ex_x:
        ex.wait_send()
    for n in range(4):
        for c in piece(n):
            c.wait_send()
    clear_pads(4)
    clear_pads(5)
    l3["ez"][:, :, 0:8, :] = jnp.zeros((16, 1, 8, 128), F32)

    ex_s.wait_recv()
    zero_outside(lev[1]["s"], 1)
    split_restrict(1, lev[1]["s"], lev[1]["tmp"], lev[1]["mid"], rz[1], lev[2]["s"])
    ex_s = exchange(lev[2]["s"], 2, (7, 6))
    rest.append(ex_s)
    pre_gi(1)
    ex_f.wait_recv()
    ex_f.wait_send()
    pre(1)
    split_restrict(1, lev[1]["r"], lev[1]["tmp"], lev[1]["mid"], rz[1], lev[2]["r"])
    ex_f = exchange(lev[2]["r"], 2, EDGE)
    ex_rho.append(exchange(lev[1]["rho"], 1, (6, 5)))
    ex_iter.append(exchange(lev[1]["x"], 1, (3, 2)))
    ex_s.wait_recv()
    zero_outside(lev[2]["s"], 2)
    pack_block(lev[2]["s"], blk_s)
    greeted(2)
    gather_s.start()
    pre_gi(2)
    ex_f.wait_recv()
    ex_f.wait_send()
    gather_s.middle()
    pre(2)
    pack_block(lev[2]["r"], blk_f)
    gather_f.start()
    ex_rho.append(exchange(lev[2]["rho"], 2, (7, 6)))
    ex_iter.append(exchange(lev[2]["x"], 2, (4, 3)))
    gather_f.middle()
    rest += [gather_s, gather_f]

    def down_pairs(src, target):
        mid = l3["mid"]

        def body(i, carry):
            v = 0.25 * (src[1 + i, 0, pl.ds(8, 32, stride=2), :] + src[1 + i, 0, pl.ds(10, 32, stride=2), :])
            mid[0, pl.ds(pl.multiple_of(32 * i, 8), 32), :] = v + 0.5 * src[1 + i, 0, pl.ds(9, 32, stride=2), :]
            return carry

        lax.fori_loop(0, 16, body, 0)
        total = dot(mid[0, 0:512, :], rz3[0]) + dot(mid[0, 32:544, :], rz3[1])
        for i in range(16):
            target[1 + i, 0, 8:40, :] = total[32 * i : 32 * i + 32]

    def down_whole(src, target):
        mid = l4["mid"]
        restrict_rows(src, l4["tmp"], mid, 8, 16, 1, 8, 48)
        total = dot(mid[0], rz4[0])
        for i in range(8):
            target[1 + i, 0, 8:24, :] = total[16 * i : 16 * i + 16]

    gather_s.finish()
    down_pairs(l3["s"], l4["s"])
    down_whole(l4["s"], l5["s"])
    for l, planes, lanes in ((3, 16, 128), (4, 16, 32), (5, 8, 16)):

        def inside(v, x, lanes=lanes):
            return jnp.where(lanes_of(v.shape) < lanes, v, 0.0)

        begin_gi(lev[l], 1, planes, lev[l]["ch"], inside)
    gather_f.finish()

    def whole_pre(l, planes):
        me = lev[l]
        d, r = me["d"], me["r"]
        begin(me, 1, planes, me["ch"])
        for k in range(3):
            smooth_step(me, d[k], r, (1, 1 + planes), d[k + 1], *FACTORS[k], r_out=r)

    def whole_residual(l, planes, f):
        me = lev[l]
        d, r = me["d"], me["r"]
        more = 2 if l == 3 else 0

        def extra(x, a, dd, new):
            s = slice(a, a + new.shape[1])
            me["x"][x + more, :, s, :] = ((d[0][x, :, s, :] + d[1][x, :, s, :]) + d[2][x, :, s, :]) + dd
            f[x, :, s, :] = (26.0 + me["s"][x, :, s, :]) * new

        smooth_step(me, d[3], r, (1, 1 + planes), r_out=r, extra=extra)

    def whole_post(l, planes):
        me = lev[l]
        d, r = me["d"], me["r"]
        span = (1, 1 + planes)
        more = 2 if l == 3 else 0
        smooth_step(me, d[0], r, span, d[1], 0.0, 1.0 / CENTER, r_out=r)
        smooth_step(me, d[1], r, span, d[2], *FACTORS[0], r_out=r)
        smooth_step(me, d[2], r, span, d[3], *FACTORS[1], r_out=r)
        al, be = FACTORS[2]

        def extra(x, a, dd, new):
            s = slice(a, a + new.shape[1])
            total = (me["x"][x + more, :, s, :] + d[0][x, :, s, :]) + (d[1][x, :, s, :] + d[2][x, :, s, :])
            me["x"][x + more, :, s, :] = (total + dd) + (al * dd + be * new)

        smooth_step(me, d[3], r, span, extra=extra)

    whole_pre(3, 16)
    whole_residual(3, 16, l3["d"][0])
    down_pairs(l3["d"][0], l4["f"])
    whole_pre(4, 16)
    whole_residual(4, 16, l4["d"][0])
    down_whole(l4["d"][0], l5["f"])

    whole_pre(5, 8)
    d5, r5 = l5["d"], l5["r"]

    def turn(x, a, dd, new):
        s = slice(a, a + new.shape[1])
        l5["x"][x, :, s, :] = ((d5[0][x, :, s, :] + d5[1][x, :, s, :]) + d5[2][x, :, s, :]) + dd

    smooth_step(l5, d5[3], r5, (1, 9), d5[0], 0.0, 1.0 / CENTER, r_out=r5, extra=turn)
    for k in range(2):
        smooth_step(l5, d5[k], r5, (1, 9), d5[k + 1], *FACTORS[k], r_out=r5)
    al, be = FACTORS[2]

    def last(x, a, dd, new):
        s = slice(a, a + new.shape[1])
        total = (l5["x"][x, :, s, :] + d5[0][x, :, s, :]) + d5[1][x, :, s, :]
        l5["x"][x, :, s, :] = (total + dd) + (al * dd + be * new)

    smooth_step(l5, d5[2], r5, (1, 9), extra=last)

    up = dot(l5["x"][1:9, 0, 8:24, :].reshape(128, 128), pz4[0])
    for i in range(8):
        l4["ez"][1 + i, 0, 8:24, :] = up[16 * i : 16 * i + 16]
    interleave(l4["ez"], l4["d"][0], 8, 1, 8, 16, 1, 8)
    whole_post(4, 16)

    e4 = l4["x"]
    up = dot(e4[1:17, 0, 8:40, :].reshape(512, 128), pz3[0]) + dot(e4[0:16, 0, 8:40, :].reshape(512, 128), pz3[1])
    for i in range(16):
        l3["ez"][i, 0, 8:40, :] = up[32 * i : 32 * i + 32]

    def rows_up(i, carry):
        a, b = l3["ez"][i, 0, 8:40, :], l3["ez"][i, 0, 7:39, :]
        l3["d"][0][1 + i, 0, pl.ds(9, 32, stride=2), :] = a
        l3["d"][0][1 + i, 0, pl.ds(8, 32, stride=2), :] = 0.5 * (a + b)
        return carry

    lax.fori_loop(0, 16, rows_up, 0)
    whole_post(3, 16)

    def correct(l, t0, row, nj):
        count = (20, 15, 12)[l]
        interleave(lev[l]["ez"], lev[l]["d"][1], count, t0, row, nj, 0, 8)
        zero_outside(lev[l]["d"][1], l, lower=False)
        ex_rho[l].wait_recv()
        ex_rho[l].wait_send()
        zero_outside(lev[l]["rho"], l)
        if l:
            ex_iter[l].wait_recv()
            ex_iter[l].wait_send()
            zero_outside(lev[l]["x"], l)

    def emit_to(l):
        def emit(x, a, v):
            lev[l]["x"][x, :, a : a + v.shape[1], :] = v
        return emit

    win = l3["x"][pl.ds(2 * gx, 7), 0, pl.ds(4 * gy, 24), :].reshape(168, 128)
    for h in range(2):
        up = dot(win, pz2[h])
        for m in range(7):
            lev[2]["ez"][2 * m + h, 0] = up[24 * m : 24 * m + 24]
    correct(2, 2, 4, 16)
    post(2, emit_to(2))

    def lift(l, first_plane, first_row, planes, rows, step):
        e, ez = lev[l + 1]["x"], lev[l]["ez"]
        for t in range(0, planes, step):
            total = None
            for z in range(ZT[l + 1]):
                v = e[first_plane + t : first_plane + t + step, z, first_row : first_row + rows, :]
                part = dot(v.reshape(step * rows, 128), pz[l][z])
                total = part if total is None else total + part
            for k in range(step):
                for z in range(ZT[l]):
                    ez[t + k, z] = total[rows * k : rows * k + rows, 128 * z : 128 * z + 128]

    lift(1, 3, 8, 16, 24, 16)
    correct(1, 1, 4, 16)
    post(1, emit_to(1))
    lift(0, 5, 13, 21, 24, 7)
    correct(0, 1, 1, 20)

    def store(i, x):
        return [
            pltpu.make_async_copy(
                l0["x"].at[pl.ds(x, 8), z, pl.ds(Y0[0], 32), :],
                out_hbm.at[pl.ds(x - X0[0], 8), :, pl.ds(128 * z, 128)],
                load_sem.at[4 + i, z],
            )
            for z in range(4)
        ]

    def after(i, x):
        for c in store(i, x):
            c.start()

    post(0, emit_to(0), after)
    for ex in rest:
        ex.wait_send()
    for i in range(4):
        for c in store(i, X0[0] + 8 * i):
            c.wait()


def pass_on(src, dst, held, sem):
    parts = [pl.ds(8 * n, 8) for n in range(4)]
    into = [pltpu.make_async_copy(src.at[p], held.at[p], sem.at[0, n]) for n, p in enumerate(parts)]
    out = [pltpu.make_async_copy(held.at[p], dst.at[p], sem.at[1, n]) for n, p in enumerate(parts)]
    for c in into:
        c.start()
    for a, b in zip(into, out):
        a.wait()
        b.start()
    for c in out:
        c.wait()


def per_device(right_side, absorption):
    scratch = []

    def vmem(*shape):
        scratch.append(pltpu.VMEM(shape, F32))

    for l in range(3):
        planes, zt, rows = PLANES[l], ZT[l], ROWS[l]
        for _ in range(3):
            vmem(planes, zt, rows, 128)
        vmem(8, zt, 8 * (CH[l] + 2), 128)
        vmem(zt, (256, 64, 16)[l], 128)
        if l == 0:
            for _ in range(6):
                vmem(planes, zt, rows, 128)
        else:
            vmem(planes, zt, rows, 128)
            vmem(*((16, 2, 24, 128), (14, 1, 24, 128))[l - 1])
    for l in range(3, 6):
        if l == 3:
            vmem(16, 1, 80, 128)
        vmem(1, (544, 128, 8)[l - 3], 128)
        if l == 3:
            vmem(18, 1, 80, 128)
            vmem(22, 1, 88, 128)
            for _ in range(7):
                vmem(18, 1, 80, 128)
    vmem(2, 1, 8, 128)
    vmem(2, 1, 8, 128)
    for shape in ((4, 128, 256), (2, 128, 512), (2, 128, 128), (1, 128, 256), (2, 128, 128), (2, 128, 128),
                  (2, 128, 128), (2, 128, 128), (1, 128, 128), (1, 128, 128)):
        vmem(*shape)
    dma = pltpu.SemaphoreType.DMA
    scratch += [dma((8, 4)), dma((12, 8)), dma((12, 8)), dma((4, 4)), dma((4, 4)), dma((2, 24)), dma((2, 24)), pltpu.SemaphoreType.REGULAR((3,))]
    result = pl.pallas_call(
        kernel,
        out_shape=jax.ShapeDtypeStruct((32, 32, 512), F32),
        in_specs=[pl.BlockSpec(memory_space=pl.ANY)] * 2,
        out_specs=pl.BlockSpec(memory_space=pl.ANY),
        scratch_shapes=scratch,
        compiler_params=pltpu.CompilerParams(
            collective_id=0, has_side_effects=True, vmem_limit_bytes=63 * 2**20
        ),
        name="vcycle",
    )(right_side, absorption)
    return pl.pallas_call(
        pass_on,
        out_shape=jax.ShapeDtypeStruct((32, 32, 512), F32),
        in_specs=[pl.BlockSpec(memory_space=pl.ANY)],
        out_specs=pl.BlockSpec(memory_space=pl.ANY),
        scratch_shapes=[pltpu.VMEM((32, 32, 512), F32), dma((2, 4))],
        name="pass_on",
    )(result)


def solution(mesh):
    spec = P("gx", "gy", None)
    return jax.shard_map(per_device, mesh=mesh, in_specs=(spec, spec), out_specs=spec, check_vma=False)
```
